128 devices in a mesh: ctx: 16 (over z_lo, y, core), tp: 4 (over x), grp: 2 (over z_hi).
Axes of the slice: x: 4, y: 4, z: 4 (z_hi: 2, z_lo: 2; z = z_hi * 2 + z_lo), core: 2. Of those that a mesh axis runs over, the one named last changes fastest.
Arguments:
- new_tokens: bfloat16 [2, 512, 4608], P('grp', None, 'ctx'), may hold values from -6 to 6
- w_query: bfloat16 [4608, 4096], P('ctx', 'tp'), may hold values from -0.25 to 0.25
- w_key: bfloat16 [4608, 2048], P('ctx', 'tp'), may hold values from -0.09375 to 0.09375
- w_value: bfloat16 [4608, 2048], P('ctx', 'tp'), may hold values from -0.09375 to 0.09375
- w_out: bfloat16 [4096, 4608], P('tp', 'ctx'), may hold values from -0.25 to 0.25
- pool_keys: bfloat16 [2, 81920, 16, 128], P('grp', 'ctx', 'tp'), may hold values from -6 to 6
- pool_values: bfloat16 [2, 81920, 16, 128], P('grp', 'ctx', 'tp'), may hold values from -6 to 6
- stretch_start: int32 [1], replicated, may hold values from 40960 to 81408
- lengths: int32 [8], replicated, may hold values from 1 to 9216, as said below
- dest_blocks: int32 [32], replicated, may hold values from 288 to 5119, as said below
Outputs:
- attn_out: bfloat16 [2, 512, 4608], P('grp', 'tp', 'ctx')
- keys_out: bfloat16 [2, 81920, 16, 128], P('grp', 'ctx', 'tp')
- values_out: bfloat16 [2, 81920, 16, 128], P('grp', 'ctx', 'tp')
The draws below stay inside these ranges and needn't reach their ends.
Inputs may be any that keep to these rules, and one draw needn't show every extreme that they name: `lengths`: the longest context is exactly 9216 in every draw, and some request has length 1. `dest_blocks`: the entries are distinct. Each block lies in the last 512 slots of its index of ctx, that is j % 5120 >= 4608 for its slots j, so no request reads it; both the first and the last such block of the pool are always named.
All inputs are finite; a program needn't handle non-finite values.
Results may differ from the reference program's by a relative error of at most 0.014.
Values may be sent and summed in bfloat16 or wider, within the bound.
A program may use at most 128 MiB of HBM per device.

```python
import jax
import jax.numpy as jnp
from jax import lax

D = 4608
HQ = 32
KVH = 16
HD = 128
ROWS = 512
REQS = 8
SLOTS_DEV = 5120
BLK = 16
SLOTS = 81920
SPEC = 64
PLANES = 640
LMAX = 9216
BLOCKS = 32
N_CTX = 16


def draw_lengths(key, part):
    key = jax.random.fold_in(key, 11)
    first_key, second_key, third_key = jax.random.split(key, 3)
    drawn = jax.random.randint(first_key, (REQS,), 1, LMAX + 1, dtype=jnp.int32)
    top_row = jax.random.randint(second_key, (), 0, REQS, dtype=jnp.int32)
    low_row = (top_row + 1 + jax.random.randint(third_key, (), 0, REQS - 1, dtype=jnp.int32)) % REQS
    drawn = drawn.at[top_row].set(LMAX)
    return drawn.at[low_row].set(1)


def draw_dest_blocks(key, part):
    key = jax.random.fold_in(key, 23)
    first_key, second_key = jax.random.split(key)
    per_device = ROWS // BLK
    total = SLOTS // SLOTS_DEV * per_device
    ranking = jax.random.permutation(first_key, total).astype(jnp.int32)
    ranking = ranking.at[0].set(-2).at[total - 1].set(-1)
    chosen = jnp.argsort(ranking, stable=True)[:BLOCKS].astype(jnp.int32)
    chosen = chosen[jax.random.permutation(second_key, BLOCKS)]
    device = chosen // per_device
    return (device * (SLOTS_DEV // BLK) + (SLOTS_DEV - ROWS) // BLK + chosen % per_device).astype(jnp.int32)


def shard_levels(rng, extent, shards, least, top_value):
    def one(axis_at, shards_of):
        steps = jax.random.uniform(jax.random.fold_in(jax.random.fold_in(rng, 6), axis_at), (shards_of,), jnp.float32, least / len(shards), top_value / len(shards))
        return jnp.repeat(jnp.exp(steps), extent[axis_at] // shards_of).reshape((-1,) + (1,) * (len(extent) - axis_at - 1))

    factor_of = one(*shards[0])
    for cut in shards[1:]:
        factor_of = factor_of * one(*cut)
    return factor_of


def scatter_about(key, extent, width, most, pieces=(), held_as=jnp.bfloat16):
    entries = jax.random.normal(key, extent, jnp.float32) * width
    if len(pieces) > 0:
        entries = shard_levels(key, extent, pieces, -0.22, 0.18) * entries
    return jnp.clip(entries, min=-most, max=most).astype(held_as)


def setup_inputs(seed: int = 0) -> dict:
    keys = jax.random.split(jax.random.key(seed), 11)
    return {
        "new_tokens": scatter_about(keys[0], (2, ROWS, D), 1.0, 6.0, ((0, 2), (2, 16))),
        "w_query": scatter_about(keys[1], (D, HQ * HD), (D // 9) ** -0.5, 0.25, ((0, 16), (1, 4))),
        "w_key": scatter_about(keys[2], (D, KVH * HD), D ** -0.5, 0.09375, ((0, 16), (1, 4))),
        "w_value": scatter_about(keys[3], (D, KVH * HD), D ** -0.5, 0.09375, ((0, 16), (1, 4))),
        "w_out": scatter_about(keys[4], (HQ * HD, D), (HQ * HD // 9) ** -0.5, 0.25, ((0, 4), (1, 16))),
        "pool_keys": scatter_about(keys[5], (2, SLOTS, KVH, HD), 1.0, 6.0, ((0, 2), (1, 16), (2, 4))),
        "pool_values": scatter_about(keys[6], (2, SLOTS, KVH, HD), 1.0, 6.0, ((0, 2), (1, 16), (2, 4))),
        "stretch_start": jax.random.randint(keys[7], (1,), SLOTS // 2, SLOTS - ROWS + 1).astype(jnp.int32),
        "lengths": draw_lengths(jax.random.fold_in(keys[10], 71), 0),
        "dest_blocks": draw_dest_blocks(jax.random.fold_in(keys[10], 71), 0),
    }


soft_cap = 50.0
query_scale = 1.0 / 12.0


def weights_of(scores, valid):
    capped = soft_cap * jnp.tanh(scores / soft_cap)
    return jnp.where(valid, jnp.exp(capped), 0.0).astype(jnp.bfloat16)


def project(tokens, w_query, w_key, w_value):
    queries = (jnp.dot(tokens, w_query, preferred_element_type=jnp.float32) * query_scale).astype(jnp.bfloat16)
    new_keys = jnp.dot(tokens, w_key, preferred_element_type=jnp.float32).astype(jnp.bfloat16)
    new_values = jnp.dot(tokens, w_value, preferred_element_type=jnp.float32).astype(jnp.bfloat16)
    return (queries.reshape(ROWS, KVH, HQ // KVH, HD), new_keys.reshape(ROWS, KVH, HD),
            new_values.reshape(ROWS, KVH, HD))


def prefix_part(queries, pool_k, pool_v, stretch_first):
    position = jnp.arange(SLOTS, dtype=jnp.int32)
    valid = (position < stretch_first)[None, None, :]

    def one_head(members):
        head_q, head_k, head_v = members
        scores = jnp.einsum("rgd,sd->rgs", head_q.astype(jnp.float32), head_k.astype(jnp.float32),
                            precision=lax.Precision.HIGHEST)
        weights = weights_of(scores, valid).astype(jnp.float32)
        numerator = jnp.einsum("rgs,sd->rgd", weights, head_v.astype(jnp.float32),
                               precision=lax.Precision.HIGHEST)
        return numerator, jnp.sum(weights, axis=-1)

    numerator, denominator = lax.map(one_head, (queries.transpose(1, 0, 2, 3), pool_k.transpose(1, 0, 2),
                                                pool_v.transpose(1, 0, 2)))
    return numerator.transpose(1, 0, 2, 3), denominator.transpose(1, 0, 2)


def cache_part(queries, pool_k, pool_v, lengths):
    key_grid = pool_k.reshape(N_CTX, PLANES, REQS, KVH, HD).transpose(3, 0, 1, 2, 4)
    value_grid = pool_v.reshape(N_CTX, PLANES, REQS, KVH, HD).transpose(3, 0, 1, 2, 4)
    position = (jnp.arange(PLANES, dtype=jnp.int32)[None, :] * N_CTX
                + jnp.arange(N_CTX, dtype=jnp.int32)[:, None])
    valid = (position[None, :, :] < lengths[:, None, None])[:, None, None, :, :]
    grouped_q = queries.reshape(REQS, SPEC, KVH, HQ // KVH, HD).transpose(2, 0, 1, 3, 4)

    def one_head(members):
        head_q, head_k, head_v = members
        scores = jnp.einsum("qsgd,cpqd->qsgcp", head_q.astype(jnp.float32), head_k.astype(jnp.float32),
                            precision=lax.Precision.HIGHEST)
        weights = weights_of(scores, valid).astype(jnp.float32)
        numerator = jnp.einsum("qsgcp,cpqd->qsgd", weights, head_v.astype(jnp.float32),
                               precision=lax.Precision.HIGHEST)
        return numerator, jnp.sum(weights, axis=(-2, -1))

    numerator, denominator = lax.map(one_head, (grouped_q, key_grid, value_grid))
    numerator = numerator.transpose(1, 2, 0, 3, 4).reshape(ROWS, KVH, HQ // KVH, HD)
    denominator = denominator.transpose(1, 2, 0, 3).reshape(ROWS, KVH, HQ // KVH)
    return numerator, denominator


def self_part(queries, new_keys, new_values, allowed):
    scores = jnp.einsum("rkgd,tkd->rkgt", queries.astype(jnp.float32), new_keys.astype(jnp.float32),
                        precision=lax.Precision.HIGHEST)
    weights = weights_of(scores, allowed[:, None, None, :]).astype(jnp.float32)
    numerator = jnp.einsum("rkgt,tkd->rkgd", weights, new_values.astype(jnp.float32),
                           precision=lax.Precision.HIGHEST)
    return numerator, jnp.sum(weights, axis=-1)


def group_output(numerator, denominator, w_out):
    heads = (numerator / denominator[..., None]).astype(jnp.bfloat16).reshape(ROWS, HQ * HD)
    return jnp.dot(heads, w_out, preferred_element_type=jnp.float32).astype(jnp.bfloat16)


def reference(new_tokens, w_query, w_key, w_value, w_out, pool_keys, pool_values, stretch_start, lengths,
              dest_blocks):
    stretch_first = stretch_start[0]
    row_ids = jnp.arange(ROWS, dtype=jnp.int32)
    request_ids = row_ids // SPEC
    prefill_q, prefill_k, prefill_v = project(new_tokens[0], w_query, w_key, w_value)
    decode_q, decode_k, decode_v = project(new_tokens[1], w_query, w_key, w_value)
    pool_num, pool_den = prefix_part(prefill_q, pool_keys[0], pool_values[0], stretch_first)
    own_num, own_den = self_part(prefill_q, prefill_k, prefill_v, row_ids[None, :] <= row_ids[:, None])
    prefill_out = group_output(pool_num + own_num, pool_den + own_den, w_out)
    cache_num, cache_den = cache_part(decode_q, pool_keys[1], pool_values[1], lengths)
    decode_allowed = (request_ids[None, :] == request_ids[:, None]) & (row_ids[None, :] <= row_ids[:, None])
    step_num, step_den = self_part(decode_q, decode_k, decode_v, decode_allowed)
    decode_out = group_output(cache_num + step_num, cache_den + step_den, w_out)
    attn_out = jnp.stack([prefill_out, decode_out])
    landing = (jnp.repeat(dest_blocks, BLK) * BLK + row_ids % BLK).astype(jnp.int32)
    stretch_slots = (stretch_first + row_ids).astype(jnp.int32)
    keys_out = jnp.stack([pool_keys[0].at[stretch_slots].set(prefill_k), pool_keys[1].at[landing].set(prefill_k)])
    values_out = jnp.stack([pool_values[0].at[stretch_slots].set(prefill_v),
                            pool_values[1].at[landing].set(prefill_v)])
    return attn_out, keys_out, values_out
```

```python
import jax
import jax.numpy as jnp
from jax import lax
from jax.experimental import pallas as pl
from jax.experimental.pallas import tpu as pltpu
from jax.sharding import PartitionSpec as P

HD = 128
GROUPED = 2
BLK = 16
REQS = 8
ROWS = 512
SLOTS_DEV = 5120
HEADS = 4
CHIPS = 8
SHARE = 32
UNIT = GROUPED * SHARE
MSG = UNIT + 16
DEINT = 512
CHUNK = 1024
STEPS = SLOTS_DEV // CHUNK
MODEL = 288
LOG2E = 1.4426950408889634

soft_cap = 50.0
query_scale = 1.0 / 12.0
bf16 = jnp.bfloat16
f32 = jnp.float32


def weights_of(scores):
    return jnp.exp2(jnp.tanh(scores * (1.0 / soft_cap)) * (soft_cap * LOG2E))


def pack_den(den):
    high = den.astype(bf16)
    low = (den - high.astype(f32)).astype(bf16)
    return jnp.concatenate([high, low], axis=-2)


def layer_kernel(
    start_ref, len_ref, tok_ref, wq_ref, wk_ref, wv_ref, wo_ref, pool_k, pool_v,
    out_ref, kv_out,
    kbuf, vbuf, kfl, vfl, kh, vh, acc,
    st1, cx1, sn1, rs1, qfull, kvown, kvgot, kvfull, kself, vself, kvfl,
    st3, cx3, sn3, rs3, hfull, oacc, st5, rs5,
    in_sem, out_sem, cx1_s, cx1_r, rs1_s, rs1_r, ag_s, ag_r, fw_s, fw_r, gr_s, gr_r,
    cx3_s, cx3_r, rs3_s, rs3_r, p5_s, p5_r,
):
    ctx = lax.axis_index("ctx")
    tp = lax.axis_index("tp")
    grp = lax.axis_index("grp")
    chip = ctx // 2
    core = lax.rem(ctx, 2)
    other = 1 - core
    sibling = {"ctx": 2 * chip + other}
    twin = {"grp": 1 - grp}

    def peer(d):
        return lax.rem(chip + d, CHIPS)

    def on_chip(k):
        return {"ctx": 2 * k + core}

    def remote(src, dst, send, recv, device):
        return pltpu.make_async_remote_copy(
            src_ref=src, dst_ref=dst, send_sem=send, recv_sem=recv, device_id=device,
            device_id_type=pl.DeviceIdType.MESH,
        )

    rows = DEINT * HEADS
    parts = SLOTS_DEV // DEINT

    def pool_in(j, which):
        src, dst = ((pool_k, kbuf), (pool_v, vbuf))[which]
        at = pl.ds(pl.multiple_of(j * rows, rows), rows)
        return pltpu.make_async_copy(src.at[at], dst.at[at], in_sem.at[which, j])

    @pl.loop(0, parts)
    def _(j):
        pool_in(j, 0).start()
        pool_in(j, 1).start()

    barrier = pltpu.get_barrier_semaphore()

    def greet(device):
        pl.semaphore_signal(barrier, inc=1, device_id=device, device_id_type=pl.DeviceIdType.MESH)

    greet(sibling)
    greet(twin)
    for d in range(1, CHIPS):
        greet(on_chip(peer(d)))
    for d in range(1, 4):
        greet({"tp": lax.rem(tp + d, 4)})
    pl.semaphore_wait(barrier, 2 + CHIPS - 1 + 3)

    def cx1_copy(u):
        return remote(st1.at[u, other], cx1.at[u], cx1_s.at[u], cx1_r.at[u], sibling)

    def rs1_send(u, k):
        return remote(sn1.at[u, k], rs1.at[u, chip], rs1_s.at[u, k], rs1_r.at[u, chip], on_chip(k))

    def rs1_recv(u, k):
        return remote(rs1.at[u, k], rs1.at[u, k], rs1_s.at[u, k], rs1_r.at[u, k], on_chip(k))

    def full_at(u, k, p):
        return qfull.at[u, k, p]

    def ag_send(ref, u, k):
        return remote(ref.at[chip, core], ref.at[chip, core], ag_s.at[u, k], ag_r.at[u, chip], on_chip(k))

    def ag_recv(ref, u, k):
        return remote(ref.at[k, core], ref.at[k, core], ag_s.at[u, k], ag_r.at[u, k], on_chip(k))

    def fw_send(ref, u, k):
        return remote(ref.at[k, core], ref.at[k, core], fw_s.at[u, k], fw_r.at[u, k], sibling)

    def fw_recv(ref, u, k):
        return remote(ref.at[k, other], ref.at[k, other], fw_s.at[u, k], fw_r.at[u, k], sibling)

    def share_out(ref, u):
        for d in range(1, CHIPS):
            ag_send(ref, u, peer(d)).start()
        fw_send(ref, u, chip).start()

    def forward(ref, u):
        @pl.loop(1, CHIPS)
        def _(d):
            k = peer(d)
            ag_recv(ref, u, k).wait_recv()
            fw_send(ref, u, k).start()

    def gathered(ref, u):
        @pl.loop(0, CHIPS)
        def _(k):
            fw_recv(ref, u, k).wait_recv()

    def shared_done(ref, u):
        @pl.loop(1, CHIPS)
        def _(d):
            ag_send(ref, u, peer(d)).wait_send()

        @pl.loop(0, CHIPS)
        def _(k):
            fw_send(ref, u, k).wait_send()

    sources = [(wq_ref, h * 256) for h in range(4)] + [
        (wk_ref, 0), (wk_ref, 256), (wv_ref, 0), (wv_ref, 256)]
    for u, (w, at) in enumerate(sources):
        part = lax.dot_general(
            tok_ref[...], w[:, at:at + 256], (((0,), (0,)), ((), ())), preferred_element_type=f32
        ).astype(bf16)
        for g in range(2):
            piece = part[:, g * HD:(g + 1) * HD].reshape(CHIPS, 2, SHARE, HD)
            for p in range(2):
                st1[u, p, :, g * SHARE:(g + 1) * SHARE, :] = piece[:, p]
        cx1_copy(u).start()

    def reduce_cores(u):
        cx1_copy(u).wait_recv()
        both = (st1[u, core].astype(f32) + cx1[u].astype(f32)).astype(bf16)
        sn1[u] = both
        rs1[u, chip] = sn1[u, chip]
        for d in range(1, CHIPS):
            rs1_send(u, peer(d)).start()

    def total1(u):
        @pl.loop(1, CHIPS)
        def _(d):
            rs1_recv(u, peer(d)).wait_recv()

        total = rs1[u, 0].astype(f32)
        for k in range(1, CHIPS):
            total = total + rs1[u, k].astype(f32)
        return total

    def finish_query(u):
        qfull[u, chip, core] = (total1(u) * query_scale).astype(bf16)
        share_out(qfull.at[u], u)

    lane_row = lax.broadcasted_iota(jnp.int32, (REQS, HD), 0)
    limits = jnp.zeros((REQS, HD), jnp.int32)
    for r in range(REQS):
        limits = jnp.where(lane_row == r, len_ref[r], limits)
    limits = jnp.where(grp == 0, start_ref[0], limits)

    def deint(j):
        pool_in(j, 0).wait()
        pool_in(j, 1).wait()
        at = pl.ds(pl.multiple_of(j * rows, rows), rows)
        kfl[...] = kbuf[at].astype(f32)
        vfl[...] = vbuf[at].astype(f32)
        slot = j * DEINT + lax.broadcasted_iota(jnp.int32, (DEINT // REQS, REQS, HD), 0) * REQS \
            + lax.broadcasted_iota(jnp.int32, (DEINT // REQS, REQS, HD), 1)
        position = jnp.where(grp == 0, ctx * SLOTS_DEV + slot, ctx + 16 * (slot // REQS))
        seen = (position < limits[None]).reshape(DEINT, HD)
        ones = jnp.where(seen, 1.0, 0.0).astype(bf16)
        to = pl.ds(pl.multiple_of(j * DEINT, DEINT), DEINT)
        for h in range(HEADS):
            kh[h, to, :] = kfl[pl.ds(h, DEINT, stride=HEADS)].astype(bf16)
            vh[h, to, 0:HD] = jnp.where(seen, vfl[pl.ds(h, DEINT, stride=HEADS)], 0.0).astype(bf16)
            vh[h, to, HD:2 * HD] = ones

    def deint_range(first, last):
        @pl.loop(first, last)
        def _(j):
            deint(j)

    deint_range(0, 2)
    for u in range(4):
        reduce_cores(u)
    deint_range(2, 5)
    finish_query(0)
    finish_query(1)
    deint_range(5, 7)
    finish_query(2)
    finish_query(3)
    for u in range(4, 8):
        reduce_cores(u)
    forward(qfull.at[0], 0)
    deint_range(7, parts)
    acc[...] = jnp.zeros_like(acc)
    kself[...] = jnp.zeros_like(kself)
    vself[...] = jnp.zeros_like(vself)
    gathered(qfull.at[0], 0)

    def queries_of(h):
        return qfull[h].reshape(ROWS * GROUPED, HD)

    def rowkeys(width):
        row = lax.broadcasted_iota(jnp.int32, (ROWS * GROUPED, width), 0)
        return jnp.where(grp == 0, 0, row // (2 * UNIT))

    def attend(h, j):
        at = pl.ds(pl.multiple_of(j * CHUNK, CHUNK), CHUNK)
        scores = lax.dot_general(
            queries_of(h), kh[h, at, :], (((1,), (1,)), ((), ())), preferred_element_type=f32
        )
        column = lax.broadcasted_iota(jnp.int32, (ROWS * GROUPED, CHUNK), 1)
        slotkey = jnp.where(grp == 0, 0, lax.rem(column, REQS))
        weights = jnp.where(rowkeys(CHUNK) == slotkey, weights_of(scores), 0.0).astype(bf16)
        acc[h] += jnp.dot(weights, vh[h, at, :], preferred_element_type=f32)

    def attend_self(h):
        scores = lax.dot_general(
            queries_of(h), kself[h], (((1,), (1,)), ((), ())), preferred_element_type=f32
        )
        index = lax.broadcasted_iota(jnp.int32, (ROWS * GROUPED, HD), 0)
        row = SHARE * (index // UNIT) + lax.rem(index, SHARE)
        key = SHARE * ctx + lax.broadcasted_iota(jnp.int32, (ROWS * GROUPED, HD), 1)
        mine = jnp.where(grp == 0, 0, ctx // 2)
        allowed = (key <= row) & (rowkeys(HD) == mine)
        weights = jnp.where(allowed, weights_of(scores), 0.0).astype(bf16)
        acc[h] += jnp.dot(weights, vself[h], preferred_element_type=f32)

    def cx3_copy(h):
        return remote(st3.at[h, other], cx3.at[h], cx3_s.at[h], cx3_r.at[h], sibling)

    def rs3_send(h, k):
        return remote(sn3.at[h, k], rs3.at[h, chip], rs3_s.at[h, k], rs3_r.at[h, chip], on_chip(k))

    def rs3_recv(h, k):
        return remote(rs3.at[h, k], rs3.at[h, k], rs3_s.at[h, k], rs3_r.at[h, k], on_chip(k))

    lane8 = lax.broadcasted_iota(jnp.int32, (2 * CHIPS, 8, HD), 2) // 16

    def hand_over(h):
        num = acc[h, :, 0:HD].astype(bf16).reshape(CHIPS, 2, UNIT, HD)
        den = acc[h, :, HD:2 * HD].reshape(2 * CHIPS, 8, 8, HD)
        small = den[:, 0]
        for a in range(1, 8):
            small = jnp.where(lane8 == a, den[:, a], small)
        small = pack_den(small).reshape(CHIPS, 2, 16, HD)
        for p in range(2):
            st3[h, p, :, 0:UNIT, :] = num[:, p]
            st3[h, p, :, UNIT:MSG, :] = small[:, p]
        cx3_copy(h).start()

    def den_of(block):
        return block[:, UNIT:UNIT + 8].astype(f32) + block[:, UNIT + 8:MSG].astype(f32)

    def reduce_cores3(h):
        cx3_copy(h).wait_recv()
        mine = st3[h, core]
        got = cx3[h]
        sn3[h, :, 0:UNIT, :] = (mine[:, 0:UNIT].astype(f32) + got[:, 0:UNIT].astype(f32)).astype(bf16)
        sn3[h, :, UNIT:MSG, :] = pack_den(den_of(mine) + den_of(got))
        rs3[h, chip] = sn3[h, chip]
        for d in range(1, CHIPS):
            rs3_send(h, peer(d)).start()

    def finish_heads(h):
        @pl.loop(1, CHIPS)
        def _(d):
            rs3_recv(h, peer(d)).wait_recv()

        got = rs3[h]
        num = jnp.sum(got[:, 0:UNIT].astype(f32), axis=0)
        den = jnp.sum(den_of(got), axis=0)
        wide = jnp.concatenate(
            [jnp.broadcast_to(den[:, 16 * a:16 * a + 1], (8, HD)) for a in range(8)], axis=0)
        hfull[h, chip, core] = (num / wide).astype(bf16)
        share_out(hfull.at[h], h + 5)

    def finish_kv():
        for u in range(4, 8):
            total = total1(u).astype(bf16)
            for half in range(2):
                h = 2 * (u % 2) + half
                piece = total[half * SHARE:(half + 1) * SHARE]
                if u < 6:
                    kself[h, 0:SHARE, :] = piece
                    kvfl[0, pl.ds(h, SHARE, stride=HEADS), :] = piece.astype(f32)
                else:
                    vself[h, 0:SHARE, 0:HD] = piece
                    vself[h, 0:SHARE, HD:2 * HD] = jnp.ones((SHARE, HD), bf16)
                    kvfl[1, pl.ds(h, SHARE, stride=HEADS), :] = piece.astype(f32)
        kvown[...] = kvfl[...].astype(bf16)
        remote(kvown, kvgot, gr_s, gr_r, twin).start()

    def share_kv():
        remote(kvown, kvgot, gr_s, gr_r, twin).wait_recv()
        kvfull[chip, core] = jnp.where(grp == 0, kvown[...].astype(f32), kvgot[...].astype(f32)).astype(bf16)
        share_out(kvfull, 4)

    kv_store = pltpu.make_async_copy(kvfull, kv_out, out_sem)

    @pl.loop(0, HEADS * STEPS)
    def _(it):
        h = it // STEPS
        j = lax.rem(it, STEPS)

        @pl.when((h == 0) & (j >= 1) & (j <= 3))
        def _():
            forward(qfull.at[j], j)

        @pl.when((h == 0) & (j == 4))
        def _():
            finish_kv()

        @pl.when((h >= 1) & (j == 0))
        def _():
            gathered(qfull.at[h], h)

        @pl.when((h >= 1) & (j == 1))
        def _():
            reduce_cores3(h - 1)

        @pl.when((h >= 1) & (j == 3))
        def _():
            finish_heads(h - 1)

        @pl.when((h >= 1) & (j == 4))
        def _():
            forward(hfull.at[h - 1], h + 4)

        @pl.when((h == 1) & (j == 2))
        def _():
            share_kv()

        @pl.when((h == 2) & (j == 2))
        def _():
            forward(kvfull, 4)

        @pl.when((h == 3) & (j == 2))
        def _():
            gathered(kvfull, 4)
            kv_store.start()

        attend(h, j)

        @pl.when(j == STEPS - 1)
        def _():
            attend_self(h)
            hand_over(h)

    def project(h):
        heads = hfull[h].reshape(2 * CHIPS, 2, SHARE, HD)
        lhs = jnp.concatenate([heads[:, 0].reshape(ROWS, HD), heads[:, 1].reshape(ROWS, HD)], axis=1)
        return lax.dot_general(
            lhs, wo_ref[:, h * 256:(h + 1) * 256], (((1,), (1,)), ((), ())), preferred_element_type=f32
        )

    reduce_cores3(HEADS - 1)
    for h in range(HEADS - 1):
        gathered(hfull.at[h], h + 5)
    total = project(0) + project(1) + project(2)
    oacc[...] = total
    finish_heads(HEADS - 1)
    forward(hfull.at[HEADS - 1], HEADS + 4)
    gathered(hfull.at[HEADS - 1], HEADS + 4)
    oacc[...] += project(HEADS - 1)
    st5[...] = oacc[...].astype(bf16).reshape(4, ROWS // 4, MODEL)

    def p5_copy(d):
        to = lax.rem(tp + d, 4)
        return remote(st5.at[to], rs5.at[d - 1], p5_s.at[d - 1], p5_r.at[d - 1], {"tp": to})

    for d in range(1, 4):
        p5_copy(d).start()
    own = oacc[pl.ds(pl.multiple_of(tp * (ROWS // 4), ROWS // 4), ROWS // 4), :]
    for d in range(1, 4):
        p5_copy(d).wait_recv()
        own = own + rs5[d - 1].astype(f32)
    out_ref[...] = own.astype(bf16)

    @pl.loop(0, 8)
    def _(u):
        cx1_copy(u).wait_send()

        @pl.loop(1, CHIPS)
        def _(d):
            rs1_send(u, peer(d)).wait_send()

    @pl.loop(0, HEADS)
    def _(h):
        cx3_copy(h).wait_send()
        shared_done(qfull.at[h], h)
        shared_done(hfull.at[h], h + 5)

        @pl.loop(1, CHIPS)
        def _(d):
            rs3_send(h, peer(d)).wait_send()

    shared_done(kvfull, 4)
    remote(kvown, kvgot, gr_s, gr_r, twin).wait_send()
    for d in range(1, 4):
        p5_copy(d).wait_send()
    kv_store.wait()


def layer(start, lengths, tok, wq, wk, wv, wo, pool_k, pool_v):
    vmem, dma = pltpu.VMEM, pltpu.SemaphoreType.DMA
    inside = pl.BlockSpec(memory_space=pltpu.VMEM)
    outside = pl.BlockSpec(memory_space=pl.ANY)
    small = pl.BlockSpec(memory_space=pltpu.SMEM)
    share = (2 * HEADS, CHIPS, UNIT, HD)
    msg = (HEADS, CHIPS, MSG, HD)
    return pl.pallas_call(
        layer_kernel,
        name="layer",
        out_shape=(
            jax.ShapeDtypeStruct((ROWS // 4, MODEL), bf16),
            jax.ShapeDtypeStruct((CHIPS, 2, 2, SHARE * HEADS, HD), bf16),
        ),
        in_specs=[small, small] + [inside] * 5 + [outside] * 2,
        out_specs=(inside, outside),
        scratch_shapes=[
            vmem((SLOTS_DEV * HEADS, HD), bf16),
            vmem((SLOTS_DEV * HEADS, HD), bf16),
            vmem((DEINT * HEADS, HD), f32),
            vmem((DEINT * HEADS, HD), f32),
            vmem((HEADS, SLOTS_DEV, HD), bf16),
            vmem((HEADS, SLOTS_DEV, 2 * HD), bf16),
            vmem((HEADS, ROWS * GROUPED, 2 * HD), f32),
            vmem((2 * HEADS, 2, CHIPS, UNIT, HD), bf16),
            vmem(share, bf16),
            vmem(share, bf16),
            vmem(share, bf16),
            vmem((HEADS, CHIPS, 2, UNIT, HD), bf16),
            vmem((2, SHARE * HEADS, HD), bf16),
            vmem((2, SHARE * HEADS, HD), bf16),
            vmem((CHIPS, 2, 2, SHARE * HEADS, HD), bf16),
            vmem((HEADS, HD, HD), bf16),
            vmem((HEADS, HD, 2 * HD), bf16),
            vmem((2, SHARE * HEADS, HD), f32),
            vmem((HEADS, 2, CHIPS, MSG, HD), bf16),
            vmem(msg, bf16),
            vmem(msg, bf16),
            vmem(msg, bf16),
            vmem((HEADS, CHIPS, 2, UNIT, HD), bf16),
            vmem((ROWS, MODEL), f32),
            vmem((4, ROWS // 4, MODEL), bf16),
            vmem((3, ROWS // 4, MODEL), bf16),
            dma((2, SLOTS_DEV // DEINT)),
            dma(()),
            dma((8,)), dma((8,)),
            dma((8, CHIPS)), dma((8, CHIPS)),
            dma((9, CHIPS)), dma((9, CHIPS)),
            dma((9, CHIPS)), dma((9, CHIPS)),
            dma(()), dma(()),
            dma((HEADS,)), dma((HEADS,)),
            dma((HEADS, CHIPS)), dma((HEADS, CHIPS)),
            dma((3,)), dma((3,)),
        ],
        compiler_params=pltpu.CompilerParams(
            collective_id=0, has_side_effects=True, vmem_limit_bytes=60 * 2**20),
        cost_estimate=pl.CostEstimate(
            flops=22 * 10**9, bytes_accessed=14 * 2**20, transcendentals=42 * 10**6),
    )(start, lengths, tok, wq, wk, wv, wo, pool_k, pool_v)


COPIES = 8


def store_kernel(where_ref, first_ref, kv, pool_k, pool_v, keys_out, values_out, copy_sem, row_sem):
    span = SLOTS_DEV // COPIES

    def whole(which, i):
        src, dst = ((pool_k, keys_out), (pool_v, values_out))[which]
        return pltpu.make_async_copy(
            src.at[pl.ds(i * span, span)], dst.at[pl.ds(i * span, span)], copy_sem.at[which, i])

    for i in range(COPIES):
        for which in range(2):
            whole(which, i).start()
    for i in range(COPIES):
        for which in range(2):
            whole(which, i).wait()

    def block(b, which):
        dst = (keys_out, values_out)[which]
        return pltpu.make_async_copy(
            kv.at[b // 4, lax.rem(b // 2, 2), which, pl.ds(lax.rem(b, 2) * BLK, BLK)],
            dst.at[pl.ds(where_ref[b] - first_ref[0], BLK)], row_sem.at[which, b])

    def inside(b):
        at = where_ref[b] - first_ref[0]
        return (at >= 0) & (at <= SLOTS_DEV - BLK)

    def across(b):
        at = where_ref[b] - first_ref[0]
        return ((at > -BLK) & (at < 0)) | ((at > SLOTS_DEV - BLK) & (at < SLOTS_DEV))

    blocks = ROWS // BLK

    @pl.loop(0, blocks)
    def _(b):
        @pl.when(inside(b))
        def _():
            block(b, 0).start()
            block(b, 1).start()

        @pl.when(across(b))
        def _():
            @pl.loop(0, BLK)
            def _(i):
                at = where_ref[b] - first_ref[0] + i

                @pl.when((at >= 0) & (at < SLOTS_DEV))
                def _():
                    for which in range(2):
                        row = pltpu.make_async_copy(
                            kv.at[b // 4, lax.rem(b // 2, 2), which,
                                  pl.ds(lax.rem(b, 2) * BLK + i, 1)],
                            (keys_out, values_out)[which].at[pl.ds(at, 1)],
                            row_sem.at[which, b])
                        row.start()
                        row.wait()

    @pl.loop(0, blocks)
    def _(b):
        @pl.when(inside(b))
        def _():
            block(b, 0).wait()
            block(b, 1).wait()


def store(where, first, kv, pool_k, pool_v):
    dma = pltpu.SemaphoreType.DMA
    outside = pl.BlockSpec(memory_space=pl.ANY)
    small = pl.BlockSpec(memory_space=pltpu.SMEM)
    shape = jax.ShapeDtypeStruct((SLOTS_DEV, HEADS, HD), bf16)
    return pl.pallas_call(
        store_kernel,
        name="store",
        out_shape=(shape, shape),
        in_specs=[small, small] + [outside] * 3,
        out_specs=(outside, outside),
        scratch_shapes=[dma((2, COPIES)), dma((2, ROWS // BLK))],
        cost_estimate=pl.CostEstimate(flops=0, bytes_accessed=21 * 2**20, transcendentals=0),
    )(where, first, kv, pool_k, pool_v)


def body(
    new_tokens, w_query, w_key, w_value, w_out, pool_keys, pool_values, stretch_start, lengths, dest_blocks
):
    flat = (SLOTS_DEV * HEADS, HD)
    pool_k = pool_keys.reshape(flat)
    pool_v = pool_values.reshape(flat)
    out, kv = layer(
        stretch_start, lengths, new_tokens[0].T, w_query, w_key, w_value, w_out.T, pool_k, pool_v)
    blocks = jnp.arange(ROWS // BLK, dtype=jnp.int32) * BLK
    where = jnp.where(lax.axis_index("grp") == 0, stretch_start[0] + blocks, dest_blocks * BLK)
    first = (lax.axis_index("ctx") * SLOTS_DEV).astype(jnp.int32).reshape(1)
    kv = kv.reshape(CHIPS, 2, 2, SHARE, HEADS, HD)
    keys_out, values_out = store(where, first, kv, pool_keys[0], pool_values[0])
    return out[None], keys_out[None], values_out[None]


def solution(mesh):
    return jax.shard_map(
        body,
        mesh=mesh,
        in_specs=(
            P("grp", None, "ctx"),
            P("ctx", "tp"),
            P("ctx", "tp"),
            P("ctx", "tp"),
            P("tp", "ctx"),
            P("grp", "ctx", "tp", None),
            P("grp", "ctx", "tp", None),
            P(),
            P(),
            P(),
        ),
        out_specs=(P("grp", "tp", "ctx"), P("grp", "ctx", "tp", None), P("grp", "ctx", "tp", None)),
        check_vma=False,
    )
```

```python
import jax
import jax.numpy as jnp
from jax import lax
from jax.experimental import pallas as pl
from jax.experimental.pallas import tpu as pltpu
from jax.sharding import PartitionSpec as P

HD = 128
GROUPED = 2
BLK = 16
REQS = 8
ROWS = 512
SLOTS_DEV = 5120
HEADS = 4
CHIPS = 8
SHARE = 32
UNIT = GROUPED * SHARE
MSG = UNIT + 16
DEINT = 512
PIECE = 128
CHUNK = 1280
CHUNKS = 2
STEPS = SLOTS_DEV // (CHUNK * CHUNKS)
MODEL = 288
LOG2E = 1.4426950408889634

soft_cap = 50.0
query_scale = 1.0 / 12.0
bf16 = jnp.bfloat16
f32 = jnp.float32


def weights_of(scores):
    return jnp.exp2(jnp.tanh(scores * (1.0 / soft_cap)) * (soft_cap * LOG2E))


def pack_den(den):
    high = den.astype(bf16)
    low = (den - high.astype(f32)).astype(bf16)
    return jnp.concatenate([high, low], axis=-2)


def layer_kernel(
    start_ref, len_ref, tok_ref, wq_ref, wk_ref, wv_ref, wo_ref, pool_k, pool_v,
    out_ref, kv_out,
    kbuf, vbuf, kfl, vfl, kh, vh, ones, acc, meets,
    st1, cx1, sn1, rs1, qfull, kvown, kvgot, kvfull, kself, vself, kvfl,
    st3, cx3, sn3, rs3, hfull, wo_got, oacc, st5, rs5,
    in_sem, out_sem, cx1_s, cx1_r, rs1_s, rs1_r, agq_s, agq_r, fwq_s, fwq_r, agk_s, agk_r, fwk_s, fwk_r,
    agh_s, agh_r, gr_s, gr_r, wo_s, wo_r,
    cx3_s, cx3_r, rs3_s, rs3_r, p5_s, p5_r,
):
    ctx = lax.axis_index("ctx")
    tp = lax.axis_index("tp")
    grp = lax.axis_index("grp")
    chip = ctx // 2
    core = lax.rem(ctx, 2)
    other = 1 - core
    sibling = {"ctx": 2 * chip + other}
    twin = {"grp": 1 - grp}

    def peer(d):
        return lax.rem(chip + d, CHIPS)

    def on_chip(k):
        return {"ctx": 2 * k + core}

    def remote(src, dst, send, recv, device):
        return pltpu.make_async_remote_copy(
            src_ref=src, dst_ref=dst, send_sem=send, recv_sem=recv, device_id=device,
            device_id_type=pl.DeviceIdType.MESH,
        )

    rows = DEINT * HEADS
    parts = SLOTS_DEV // DEINT

    def pool_in(j, which):
        src, dst = ((pool_k, kbuf), (pool_v, vbuf))[which]
        at = pl.ds(pl.multiple_of(j * rows, rows), rows)
        return pltpu.make_async_copy(src.at[at], dst.at[at], in_sem.at[which, j])

    @pl.loop(0, parts)
    def _(j):
        pool_in(j, 0).start()
        pool_in(j, 1).start()

    barrier = pltpu.get_barrier_semaphore()

    def greet(device):
        pl.semaphore_signal(barrier, inc=1, device_id=device, device_id_type=pl.DeviceIdType.MESH)

    greet(sibling)
    greet(twin)
    for d in range(1, CHIPS):
        greet(on_chip(peer(d)))
    for d in range(1, 4):
        greet({"tp": lax.rem(tp + d, 4)})
        greet({"ctx": 2 * chip + other, "tp": lax.rem(tp + d, 4)})

    def cx1_copy(u):
        return remote(st1.at[u, other], cx1.at[u], cx1_s.at[u], cx1_r.at[u], sibling)

    seven = pl.ds(0, CHIPS - 1)

    def rs1_send(u, k):
        return remote(sn1.at[u, k], rs1.at[u, chip], rs1_s, rs1_r.at[u], on_chip(k))

    def rs1_all(u):
        return remote(sn1.at[u, seven], rs1.at[u, seven], rs1_s, rs1_r.at[u], sibling)

    def ag_send(buf, u, k):
        ref, send, recv, _, _ = buf
        return remote(ref.at[u, chip, core], ref.at[u, chip, core], send, recv.at[u], on_chip(k))

    def ag_all(buf, u):
        ref, send, recv, _, _ = buf
        return remote(ref.at[u, seven, core], ref.at[u, seven, core], send, recv.at[u], sibling)

    def fw_send(buf, u):
        ref, _, _, send, recv = buf
        return remote(ref.at[u, :, core], ref.at[u, :, core], send.at[u], recv.at[u], sibling)

    def share_out(buf, u):
        for d in range(1, CHIPS):
            ag_send(buf, u, peer(d)).start()

    def forward(buf, u):
        ag_all(buf, u).wait_recv()
        fw_send(buf, u).start()

    def gathered(buf, u):
        ref, _, _, send, recv = buf
        remote(ref.at[u, :, other], ref.at[u, :, other], send.at[u], recv.at[u], sibling).wait_recv()

    def shared_done(buf, u):
        ag_all(buf, u).wait_send()
        fw_send(buf, u).wait_send()

    queries = (qfull, agq_s, agq_r, fwq_s, fwq_r)
    new_rows = (kvfull, agk_s, agk_r, fwk_s, fwk_r)
    heads_out = (hfull, agh_s, agh_r, None, None)

    wo_copy = remote(wo_ref, wo_got, wo_s, wo_r, sibling)

    def project_in(w_ref, first):
        part = lax.dot_general(
            tok_ref[...], w_ref[...], (((0,), (0,)), ((), ())), preferred_element_type=f32
        ).astype(bf16)
        for n in range(part.shape[1] // HD):
            piece = part[:, n * HD:(n + 1) * HD].reshape(CHIPS, 2, SHARE, HD)
            u, g = first + n // 2, n % 2
            for p in range(2):
                st1[u, p, :, g * SHARE:(g + 1) * SHARE, :] = piece[:, p]

    project_in(wq_ref, 0)
    pl.semaphore_wait(barrier, 2 + CHIPS - 1 + 6)
    for u in range(4):
        cx1_copy(u).start()
    project_in(wk_ref, 4)
    project_in(wv_ref, 6)
    for u in range(4, 8):
        cx1_copy(u).start()
    wo_copy.start()

    def reduce_cores(u):
        cx1_copy(u).wait_recv()
        both = (st1[u, core].astype(f32) + cx1[u].astype(f32)).astype(bf16)
        sn1[u] = both
        rs1[u, chip] = sn1[u, chip]
        for d in range(1, CHIPS):
            rs1_send(u, peer(d)).start()

    def total1(u):
        rs1_all(u).wait_recv()
        total = rs1[u, 0].astype(f32)
        for k in range(1, CHIPS):
            total = total + rs1[u, k].astype(f32)
        return total

    def finish_query(u):
        qfull[u, chip, core] = (total1(u) * query_scale).astype(bf16)
        share_out(queries, u)

    lane_row = lax.broadcasted_iota(jnp.int32, (REQS, HD), 0)
    limits = jnp.zeros((REQS, HD), jnp.int32)
    for r in range(REQS):
        limits = jnp.where(lane_row == r, len_ref[r], limits)
    limits = jnp.where(grp == 0, start_ref[0] - ctx * SLOTS_DEV - lane_row, limits - ctx)
    plane_step = jnp.where(grp == 0, REQS, 16)
    piece_planes = PIECE // REQS
    plane_of = lax.broadcasted_iota(jnp.int32, (piece_planes, REQS, HD), 0) * plane_step

    def deint(j):
        pool_in(j, 0).wait()
        pool_in(j, 1).wait()

        @pl.loop(0, DEINT // PIECE)
        def _(i):
            first = j * DEINT + i * PIECE
            at = pl.ds(pl.multiple_of(first * HEADS, PIECE * HEADS), PIECE * HEADS)
            to = pl.ds(pl.multiple_of(first, PIECE), PIECE)
            kfl[...] = kbuf[at].astype(f32)
            vfl[...] = vbuf[at].astype(f32)
            planes = plane_of + (first // REQS) * plane_step
            seen = jnp.where(planes < limits[None], 1.0, 0.0).reshape(PIECE, HD)
            ones[to, :] = seen.astype(bf16)
            for h in range(HEADS):
                kh[h, to, :] = kfl[pl.ds(h, PIECE, stride=HEADS)].astype(bf16)
                vh[h, to, :] = (vfl[pl.ds(h, PIECE, stride=HEADS)] * seen).astype(bf16)

    def deint_range(first, last):
        @pl.loop(first, last)
        def _(j):
            deint(j)

    deint_range(0, 1)
    for u in range(4):
        reduce_cores(u)
    deint_range(1, 4)
    finish_query(0)
    finish_query(1)
    deint_range(4, 5)
    finish_query(2)
    finish_query(3)
    deint_range(5, 6)
    forward(queries, 0)
    deint_range(6, parts)
    acc[...] = jnp.zeros_like(acc)
    kself[...] = jnp.zeros_like(kself)
    vself[...] = jnp.zeros_like(vself)
    gathered(queries, 0)

    def queries_of(h):
        return qfull[h].reshape(ROWS * GROUPED, HD)

    row_request = lax.broadcasted_iota(jnp.int32, (ROWS * GROUPED, HD), 0) // (2 * UNIT)
    lane_request = lax.rem(lax.broadcasted_iota(jnp.int32, (ROWS * GROUPED, HD), 1), REQS)
    meets[...] = jnp.where((grp == 0) | (row_request == lane_request), 1.0, 0.0)

    def attend(h, j):
        mask = jnp.concatenate([meets[...]] * (CHUNK // HD), axis=1)
        for n in range(CHUNKS):
            at = pl.ds(pl.multiple_of((j * CHUNKS + n) * CHUNK, CHUNK), CHUNK)
            scores = lax.dot_general(
                queries_of(h), kh[h, at, :], (((1,), (1,)), ((), ())), preferred_element_type=f32
            )
            weights = (weights_of(scores) * mask).astype(bf16)
            values = jnp.concatenate([vh[h, at, :], ones[at, :]], axis=1)
            acc[h] += jnp.dot(weights, values, preferred_element_type=f32)

    def attend_self(h):
        scores = lax.dot_general(
            queries_of(h), kself[h], (((1,), (1,)), ((), ())), preferred_element_type=f32
        )
        index = lax.broadcasted_iota(jnp.int32, (ROWS * GROUPED, HD), 0)
        row = SHARE * (index // UNIT) + lax.rem(index, SHARE)
        key = SHARE * ctx + lax.broadcasted_iota(jnp.int32, (ROWS * GROUPED, HD), 1)
        allowed = (key <= row) & ((grp == 0) | (index // (2 * UNIT) == ctx // 2))
        weights = jnp.where(allowed, weights_of(scores), 0.0).astype(bf16)
        acc[h] += jnp.dot(weights, vself[h], preferred_element_type=f32)

    def cx3_copy(h):
        return remote(st3.at[h, other], cx3.at[h], cx3_s.at[h], cx3_r.at[h], sibling)

    def rs3_send(h, k):
        return remote(sn3.at[h, k], rs3.at[h, chip], rs3_s, rs3_r.at[h], on_chip(k))

    def rs3_all(h):
        return remote(sn3.at[h, seven], rs3.at[h, seven], rs3_s, rs3_r.at[h], sibling)

    lane8 = lax.broadcasted_iota(jnp.int32, (2 * CHIPS, 8, HD), 2) // 16

    def hand_over(h):
        num = acc[h, :, 0:HD].astype(bf16).reshape(CHIPS, 2, UNIT, HD)
        den = acc[h, :, HD:2 * HD].reshape(2 * CHIPS, 8, 8, HD)
        small = den[:, 0]
        for a in range(1, 8):
            small = jnp.where(lane8 == a, den[:, a], small)
        small = pack_den(small).reshape(CHIPS, 2, 16, HD)
        for p in range(2):
            st3[h, p, :, 0:UNIT, :] = num[:, p]
            st3[h, p, :, UNIT:MSG, :] = small[:, p]
        cx3_copy(h).start()

    def den_of(block):
        return block[:, UNIT:UNIT + 8].astype(f32) + block[:, UNIT + 8:MSG].astype(f32)

    def reduce_cores3(h):
        cx3_copy(h).wait_recv()
        mine = st3[h, core]
        got = cx3[h]
        sn3[h, :, 0:UNIT, :] = (mine[:, 0:UNIT].astype(f32) + got[:, 0:UNIT].astype(f32)).astype(bf16)
        sn3[h, :, UNIT:MSG, :] = pack_den(den_of(mine) + den_of(got))
        rs3[h, chip] = sn3[h, chip]
        for d in range(1, CHIPS):
            rs3_send(h, peer(d)).start()

    def finish_heads(h):
        rs3_all(h).wait_recv()
        got = rs3[h]
        num = jnp.sum(got[:, 0:UNIT].astype(f32), axis=0)
        den = jnp.sum(den_of(got), axis=0)
        wide = jnp.concatenate(
            [jnp.broadcast_to(den[:, 16 * a:16 * a + 1], (8, HD)) for a in range(8)], axis=0)
        hfull[h, chip, core] = (num / wide).astype(bf16)
        share_out(heads_out, h)

    def finish_kv():
        for u in range(4, 8):
            total = total1(u).astype(bf16)
            for half in range(2):
                h = 2 * (u % 2) + half
                piece = total[half * SHARE:(half + 1) * SHARE]
                if u < 6:
                    kself[h, 0:SHARE, :] = piece
                    kvfl[0, pl.ds(h, SHARE, stride=HEADS), :] = piece.astype(f32)
                else:
                    vself[h, 0:SHARE, 0:HD] = piece
                    vself[h, 0:SHARE, HD:2 * HD] = jnp.ones((SHARE, HD), bf16)
                    kvfl[1, pl.ds(h, SHARE, stride=HEADS), :] = piece.astype(f32)
        kvown[...] = kvfl[...].astype(bf16)
        remote(kvown, kvgot, gr_s, gr_r, twin).start()

    def pick_kv():
        remote(kvown, kvgot, gr_s, gr_r, twin).wait_recv()
        kvfull[0, chip, core] = jnp.where(grp == 0, kvown[...].astype(f32), kvgot[...].astype(f32)).astype(bf16)

    kv_store = pltpu.make_async_copy(kvfull.at[0], kv_out, out_sem)

    @pl.loop(0, HEADS * STEPS)
    def _(it):
        h = it // STEPS
        j = lax.rem(it, STEPS)

        @pl.when(it == 0)
        def _():
            for u in range(4, 8):
                reduce_cores(u)

        @pl.when(it == 1)
        def _():
            for u in range(1, HEADS):
                forward(queries, u)

        @pl.when((h >= 1) & (j == 0))
        def _():
            gathered(queries, h)

        @pl.when(it == 2)
        def _():
            finish_kv()
            attend_self(0)
            hand_over(0)

        @pl.when(it == 3)
        def _():
            pick_kv()
            share_out(new_rows, 0)

        @pl.when((it == 3) | (it == 4) | (it == 6))
        def _():
            reduce_cores3(it // 2 - 1)

        @pl.when(it == 5)
        def _():
            finish_heads(0)
            finish_heads(1)

        @pl.when(it == 6)
        def _():
            forward(new_rows, 0)

        @pl.when(it == 7)
        def _():
            gathered(new_rows, 0)
            kv_store.start()

        attend(h, j)

        @pl.when((h >= 1) & (j == STEPS - 1))
        def _():
            attend_self(h)
            hand_over(h)

    last = HEADS - 1
    half = ROWS // 2

    def project(h):
        heads = hfull[h, :, core]
        lhs = jnp.concatenate(
            [heads[:, 0:SHARE].reshape(half, HD), heads[:, SHARE:UNIT].reshape(half, HD)], axis=1)
        for q, w_ref in enumerate((wo_ref, wo_got)):
            term = lax.dot_general(
                lhs, w_ref[:, h * 256:(h + 1) * 256], (((1,), (1,)), ((), ())), preferred_element_type=f32)
            oacc[q] = term if h == 0 else oacc[q] + term

    reduce_cores3(last)
    finish_heads(last - 1)
    wo_copy.wait_recv()
    for h in range(last - 1):
        ag_all(heads_out, h).wait_recv()
        project(h)
    finish_heads(last)
    ag_all(heads_out, last - 1).wait_recv()
    project(last - 1)
    ag_all(heads_out, last).wait_recv()
    project(last)
    st5[...] = oacc[...].astype(bf16).reshape(2, 4, UNIT, MODEL)

    def p5_send(q, t):
        return remote(st5.at[q, t], rs5.at[4 * core + tp], p5_s, p5_r,
                      {"ctx": ctx if q == 0 else 2 * chip + other, "tp": t})

    p5_all = remote(rs5.at[seven], rs5.at[seven], p5_s, p5_r, sibling)
    for d in range(1, 4):
        to = lax.rem(tp + d, 4)
        p5_send(0, to).start()
        p5_send(1, to).start()
    p5_send(1, tp).start()
    rs5[4 * core + tp] = st5[0, tp]
    p5_all.wait_recv()
    pieces = []
    for p in range(2):
        total = rs5[4 * p].astype(f32)
        for t in range(1, 4):
            total = total + rs5[4 * p + t].astype(f32)
        pieces.append(total)
    out_ref[...] = jnp.concatenate(
        [pieces[0][0:SHARE], pieces[1][0:SHARE], pieces[0][SHARE:UNIT], pieces[1][SHARE:UNIT]], axis=0)

    @pl.loop(0, 8)
    def _(u):
        cx1_copy(u).wait_send()
        rs1_all(u).wait_send()

    @pl.loop(0, HEADS)
    def _(h):
        cx3_copy(h).wait_send()
        rs3_all(h).wait_send()
        shared_done(queries, h)
        ag_all(heads_out, h).wait_send()

    shared_done(new_rows, 0)
    remote(kvown, kvgot, gr_s, gr_r, twin).wait_send()
    wo_copy.wait_send()
    p5_all.wait_send()
    kv_store.wait()


def layer(start, lengths, tok, wq, wk, wv, wo, pool_k, pool_v):
    vmem, dma = pltpu.VMEM, pltpu.SemaphoreType.DMA
    inside = pl.BlockSpec(memory_space=pltpu.VMEM)
    outside = pl.BlockSpec(memory_space=pl.ANY)
    small = pl.BlockSpec(memory_space=pltpu.SMEM)
    share = (2 * HEADS, CHIPS, UNIT, HD)
    msg = (HEADS, CHIPS, MSG, HD)
    return pl.pallas_call(
        layer_kernel,
        name="layer",
        out_shape=(
            jax.ShapeDtypeStruct((ROWS // 4, MODEL), f32),
            jax.ShapeDtypeStruct((CHIPS, 2, 2, SHARE * HEADS, HD), bf16),
        ),
        in_specs=[small, small] + [inside] * 5 + [outside] * 2,
        out_specs=(inside, outside),
        scratch_shapes=[
            vmem((SLOTS_DEV * HEADS, HD), bf16),
            vmem((SLOTS_DEV * HEADS, HD), bf16),
            vmem((PIECE * HEADS, HD), f32),
            vmem((PIECE * HEADS, HD), f32),
            vmem((HEADS, SLOTS_DEV, HD), bf16),
            vmem((HEADS, SLOTS_DEV, HD), bf16),
            vmem((SLOTS_DEV, HD), bf16),
            vmem((HEADS, ROWS * GROUPED, 2 * HD), f32),
            vmem((ROWS * GROUPED, HD), f32),
            vmem((2 * HEADS, 2, CHIPS, UNIT, HD), bf16),
            vmem(share, bf16),
            vmem(share, bf16),
            vmem(share, bf16),
            vmem((HEADS, CHIPS, 2, UNIT, HD), bf16),
            vmem((2, SHARE * HEADS, HD), bf16),
            vmem((2, SHARE * HEADS, HD), bf16),
            vmem((1, CHIPS, 2, 2, SHARE * HEADS, HD), bf16),
            vmem((HEADS, HD, HD), bf16),
            vmem((HEADS, HD, 2 * HD), bf16),
            vmem((2, SHARE * HEADS, HD), f32),
            vmem((HEADS, 2, CHIPS, MSG, HD), bf16),
            vmem(msg, bf16),
            vmem(msg, bf16),
            vmem(msg, bf16),
            vmem((HEADS, CHIPS, 2, UNIT, HD), bf16),
            vmem((MODEL, HEADS * GROUPED * HD), bf16),
            vmem((2, ROWS // 2, MODEL), f32),
            vmem((2, 4, UNIT, MODEL), bf16),
            vmem((8, UNIT, MODEL), bf16),
            dma((2, SLOTS_DEV // DEINT)),
            dma(()),
            dma((8,)), dma((8,)),
            dma(()), dma((8,)),
            dma(()), dma((HEADS,)), dma((HEADS,)), dma((HEADS,)),
            dma(()), dma((1,)), dma((1,)), dma((1,)),
            dma(()), dma((HEADS,)),
            dma(()), dma(()),
            dma(()), dma(()),
            dma((HEADS,)), dma((HEADS,)),
            dma(()), dma((HEADS,)),
            dma(()), dma(()),
        ],
        compiler_params=pltpu.CompilerParams(
            collective_id=0, has_side_effects=True, vmem_limit_bytes=60 * 2**20),
        cost_estimate=pl.CostEstimate(
            flops=22 * 10**9, bytes_accessed=14 * 2**20, transcendentals=42 * 10**6),
    )(start, lengths, tok, wq, wk, wv, wo, pool_k, pool_v)


COPIES = 8


def store_kernel(
    start_ref, dest_ref, attn, kv, pool_k, pool_v, attn_out, keys_out, values_out, held, in_sem, copy_sem, row_sem
):
    grp = lax.axis_index("grp")
    first = lax.axis_index("ctx") * SLOTS_DEV
    span = SLOTS_DEV // COPIES

    def fetch(which, i):
        at = pl.ds(i * span, span)
        return pltpu.make_async_copy((pool_k, pool_v)[which].at[at], held.at[which, at], in_sem.at[which, i])

    def put(which, i):
        at = pl.ds(i * span, span)
        return pltpu.make_async_copy(held.at[which, at], (keys_out, values_out)[which].at[at], copy_sem.at[which, i])

    for i in range(COPIES):
        for which in range(2):
            fetch(which, i).start()
    attn_out[...] = attn[...].T.astype(bf16)
    for i in range(COPIES):
        for which in range(2):
            fetch(which, i).wait()
            put(which, i).start()
    for i in range(COPIES):
        for which in range(2):
            put(which, i).wait()

    def slot(b):
        return jnp.where(grp == 0, start_ref[0] + b * BLK, dest_ref[b] * BLK) - first

    def block(b, which):
        dst = (keys_out, values_out)[which]
        return pltpu.make_async_copy(
            kv.at[b // 4, lax.rem(b // 2, 2), which, pl.ds(lax.rem(b, 2) * BLK, BLK)],
            dst.at[pl.ds(slot(b), BLK)], row_sem.at[which, b])

    def inside(b):
        at = slot(b)
        return (at >= 0) & (at <= SLOTS_DEV - BLK)

    def across(b):
        at = slot(b)
        return ((at > -BLK) & (at < 0)) | ((at > SLOTS_DEV - BLK) & (at < SLOTS_DEV))

    blocks = ROWS // BLK

    @pl.loop(0, blocks)
    def _(b):
        @pl.when(inside(b))
        def _():
            block(b, 0).start()
            block(b, 1).start()

        @pl.when(across(b))
        def _():
            @pl.loop(0, BLK)
            def _(i):
                at = slot(b) + i

                @pl.when((at >= 0) & (at < SLOTS_DEV))
                def _():
                    for which in range(2):
                        row = pltpu.make_async_copy(
                            kv.at[b // 4, lax.rem(b // 2, 2), which,
                                  pl.ds(lax.rem(b, 2) * BLK + i, 1)],
                            (keys_out, values_out)[which].at[pl.ds(at, 1)],
                            row_sem.at[which, b])
                        row.start()
                        row.wait()

    @pl.loop(0, blocks)
    def _(b):
        @pl.when(inside(b))
        def _():
            block(b, 0).wait()
            block(b, 1).wait()


def store(start, dest_blocks, attn, kv, pool_k, pool_v):
    dma = pltpu.SemaphoreType.DMA
    inside = pl.BlockSpec(memory_space=pltpu.VMEM)
    outside = pl.BlockSpec(memory_space=pl.ANY)
    small = pl.BlockSpec(memory_space=pltpu.SMEM)
    shape = jax.ShapeDtypeStruct((SLOTS_DEV, HEADS, HD), bf16)
    return pl.pallas_call(
        store_kernel,
        name="store",
        out_shape=(jax.ShapeDtypeStruct((MODEL, ROWS // 4), bf16), shape, shape),
        in_specs=[small, small, inside] + [outside] * 3,
        out_specs=(inside, outside, outside),
        scratch_shapes=[
            pltpu.VMEM((2, SLOTS_DEV, HEADS, HD), bf16),
            dma((2, COPIES)), dma((2, COPIES)), dma((2, ROWS // BLK))],
        compiler_params=pltpu.CompilerParams(vmem_limit_bytes=60 * 2**20),
        cost_estimate=pl.CostEstimate(flops=0, bytes_accessed=21 * 2**20, transcendentals=0),
    )(start, dest_blocks, attn, kv, pool_k, pool_v)


def body(
    new_tokens, w_query, w_key, w_value, w_out, pool_keys, pool_values, stretch_start, lengths, dest_blocks
):
    flat = (SLOTS_DEV * HEADS, HD)
    pool_k = pool_keys.reshape(flat)
    pool_v = pool_values.reshape(flat)
    out, kv = layer(
        stretch_start, lengths, new_tokens[0].T, w_query, w_key, w_value, w_out.T, pool_k, pool_v)
    kv = kv.reshape(CHIPS, 2, 2, SHARE, HEADS, HD)
    attn_out, keys_out, values_out = store(
        stretch_start, dest_blocks, out, kv, pool_keys[0], pool_values[0])
    return attn_out.T[None], keys_out[None], values_out[None]


def solution(mesh):
    return jax.shard_map(
        body,
        mesh=mesh,
        in_specs=(
            P("grp", None, "ctx"),
            P("ctx", "tp"),
            P("ctx", "tp"),
            P("ctx", "tp"),
            P("tp", "ctx"),
            P("grp", "ctx", "tp", None),
            P("grp", "ctx", "tp", None),
            P(),
            P(),
            P(),
        ),
        out_specs=(P("grp", "tp", "ctx"), P("grp", "ctx", "tp", None), P("grp", "ctx", "tp", None)),
        check_vma=False,
    )
```

```python
import jax
import jax.numpy as jnp
from jax import lax
from jax.experimental import pallas as pl
from jax.experimental.pallas import tpu as pltpu
from jax.sharding import PartitionSpec as P

HD = 128
GROUPED = 2
BLK = 16
REQS = 8
ROWS = 512
SLOTS_DEV = 5120
HEADS = 4
CHIPS = 8
SHARE = 32
UNIT = GROUPED * SHARE
MSG = UNIT + 16
DEINT = 512
PIECE = 128
CHUNK = 1280
CHUNKS = 2
STEPS = SLOTS_DEV // (CHUNK * CHUNKS)
MODEL = 288
LOG2E = 1.4426950408889634

soft_cap = 50.0
query_scale = 1.0 / 12.0
bf16 = jnp.bfloat16
f32 = jnp.float32


def weights_of(scores):
    return jnp.exp2(jnp.tanh(scores * (1.0 / soft_cap)) * (soft_cap * LOG2E))


def pack_den(den):
    high = den.astype(bf16)
    low = (den - high.astype(f32)).astype(bf16)
    return jnp.concatenate([high, low], axis=-2)


def layer_kernel(
    start_ref, len_ref, tok_ref, wq_ref, wk_ref, wv_ref, wo_ref, pool_k, pool_v,
    out_ref, kv_out,
    kbuf, vbuf, kfl, vfl, kh, vh, ones, acc, meets,
    st1, cx1, sn1, rs1, qfull, kvown, kvgot, kvfull, kself, vself, kvfl,
    st3, cx3, sn3, rs3, hfull, wo_got, oacc, st5, rs5,
    in_sem, out_sem, cx1_s, cx1_r, rs1_s, rs1_r, agq_s, agq_r, fwq_s, fwq_r, agk_s, agk_r, fwk_s, fwk_r,
    agh_s, agh_r, gr_s, gr_r, wo_s, wo_r,
    cx3_s, cx3_r, rs3_s, rs3_r, p5_s, p5_r,
):
    ctx = lax.axis_index("ctx")
    tp = lax.axis_index("tp")
    grp = lax.axis_index("grp")
    chip = ctx // 2
    core = lax.rem(ctx, 2)
    other = 1 - core
    sibling = {"ctx": 2 * chip + other}
    twin = {"grp": 1 - grp}

    def peer(d):
        return lax.rem(chip + d, CHIPS)

    def on_chip(k):
        return {"ctx": 2 * k + core}

    def remote(src, dst, send, recv, device):
        return pltpu.make_async_remote_copy(
            src_ref=src, dst_ref=dst, send_sem=send, recv_sem=recv, device_id=device,
            device_id_type=pl.DeviceIdType.MESH,
        )

    rows = DEINT * HEADS
    parts = SLOTS_DEV // DEINT

    def pool_in(j, which):
        src, dst = ((pool_k, kbuf), (pool_v, vbuf))[which]
        at = pl.ds(pl.multiple_of(j * rows, rows), rows)
        return pltpu.make_async_copy(src.at[at], dst.at[at], in_sem.at[which, j])

    @pl.loop(0, parts)
    def _(j):
        pool_in(j, 0).start()
        pool_in(j, 1).start()

    barrier = pltpu.get_barrier_semaphore()

    def greet(device):
        pl.semaphore_signal(barrier, inc=1, device_id=device, device_id_type=pl.DeviceIdType.MESH)

    greet(sibling)
    greet(twin)
    for d in range(1, CHIPS):
        greet(on_chip(peer(d)))
    for d in range(1, 4):
        greet({"tp": lax.rem(tp + d, 4)})
        greet({"ctx": 2 * chip + other, "tp": lax.rem(tp + d, 4)})

    def cx1_copy(u):
        return remote(st1.at[u, other], cx1.at[u], cx1_s.at[u], cx1_r.at[u], sibling)

    seven = pl.ds(0, CHIPS - 1)

    def rs1_send(u, k):
        return remote(sn1.at[u, k], rs1.at[u, chip], rs1_s, rs1_r.at[u], on_chip(k))

    def rs1_all(u):
        return remote(sn1.at[u, seven], rs1.at[u, seven], rs1_s, rs1_r.at[u], sibling)

    def ag_send(buf, u, k):
        ref, send, recv, _, _ = buf
        return remote(ref.at[u, chip, core], ref.at[u, chip, core], send, recv.at[u], on_chip(k))

    def ag_all(buf, u):
        ref, send, recv, _, _ = buf
        return remote(ref.at[u, seven, core], ref.at[u, seven, core], send, recv.at[u], sibling)

    def fw_send(buf, u):
        ref, _, _, send, recv = buf
        return remote(ref.at[u, :, core], ref.at[u, :, core], send.at[u], recv.at[u], sibling)

    def share_out(buf, u):
        for d in range(1, CHIPS):
            ag_send(buf, u, peer(d)).start()

    def forward(buf, u):
        ag_all(buf, u).wait_recv()
        fw_send(buf, u).start()

    def gathered(buf, u):
        ref, _, _, send, recv = buf
        remote(ref.at[u, :, other], ref.at[u, :, other], send.at[u], recv.at[u], sibling).wait_recv()

    def shared_done(buf, u):
        ag_all(buf, u).wait_send()
        fw_send(buf, u).wait_send()

    queries = (qfull, agq_s, agq_r, fwq_s, fwq_r)
    new_rows = (kvfull, agk_s, agk_r, fwk_s, fwk_r)
    heads_out = (hfull, agh_s, agh_r, None, None)

    wo_copy = remote(wo_ref, wo_got, wo_s, wo_r, sibling)

    def project_in(w_ref, first):
        part = lax.dot_general(
            tok_ref[...], w_ref[...], (((0,), (0,)), ((), ())), preferred_element_type=f32
        ).astype(bf16)
        for n in range(part.shape[1] // HD):
            piece = part[:, n * HD:(n + 1) * HD].reshape(CHIPS, 2, SHARE, HD)
            u, g = first + n // 2, n % 2
            for p in range(2):
                st1[u, p, :, g * SHARE:(g + 1) * SHARE, :] = piece[:, p]

    project_in(wq_ref, 0)
    pl.semaphore_wait(barrier, 2 + CHIPS - 1 + 6)
    for u in range(4):
        cx1_copy(u).start()
    project_in(wk_ref, 4)
    project_in(wv_ref, 6)
    for u in range(4, 8):
        cx1_copy(u).start()
    wo_copy.start()

    def reduce_cores(u):
        cx1_copy(u).wait_recv()
        both = (st1[u, core].astype(f32) + cx1[u].astype(f32)).astype(bf16)
        sn1[u] = both
        rs1[u, chip] = sn1[u, chip]
        for d in range(1, CHIPS):
            rs1_send(u, peer(d)).start()

    def total1(u):
        rs1_all(u).wait_recv()
        total = rs1[u, 0].astype(f32)
        for k in range(1, CHIPS):
            total = total + rs1[u, k].astype(f32)
        return total

    def finish_query(u):
        qfull[u, chip, core] = (total1(u) * query_scale).astype(bf16)
        share_out(queries, u)

    lane_row = lax.broadcasted_iota(jnp.int32, (REQS, HD), 0)
    limits = jnp.zeros((REQS, HD), jnp.int32)
    for r in range(REQS):
        limits = jnp.where(lane_row == r, len_ref[r], limits)
    limits = jnp.where(grp == 0, start_ref[0] - ctx * SLOTS_DEV - lane_row, limits - ctx)
    plane_step = jnp.where(grp == 0, REQS, 16)
    piece_planes = PIECE // REQS
    plane_of = lax.broadcasted_iota(jnp.int32, (piece_planes, REQS, HD), 0) * plane_step

    def deint(j):
        pool_in(j, 0).wait()
        pool_in(j, 1).wait()

        @pl.loop(0, DEINT // PIECE)
        def _(i):
            first = j * DEINT + i * PIECE
            at = pl.ds(pl.multiple_of(first * HEADS, PIECE * HEADS), PIECE * HEADS)
            to = pl.ds(pl.multiple_of(first, PIECE), PIECE)
            kfl[...] = kbuf[at].astype(f32)
            vfl[...] = vbuf[at].astype(f32)
            planes = plane_of + (first // REQS) * plane_step
            seen = jnp.where(planes < limits[None], 1.0, 0.0).reshape(PIECE, HD)
            ones[to, :] = seen.astype(bf16)
            for h in range(HEADS):
                kh[h, to, :] = kfl[pl.ds(h, PIECE, stride=HEADS)].astype(bf16)
                vh[h, to, :] = (vfl[pl.ds(h, PIECE, stride=HEADS)] * seen).astype(bf16)

    def deint_range(first, last):
        @pl.loop(first, last)
        def _(j):
            deint(j)

    deint_range(0, 1)
    for u in range(4):
        reduce_cores(u)
    deint_range(1, 4)
    finish_query(0)
    finish_query(1)
    deint_range(4, 5)
    finish_query(2)
    finish_query(3)
    deint_range(5, 6)
    for u in range(4, 8):
        reduce_cores(u)
    forward(queries, 0)
    deint_range(6, parts)
    acc[...] = jnp.zeros_like(acc)
    kself[...] = jnp.zeros_like(kself)
    vself[...] = jnp.zeros_like(vself)
    gathered(queries, 0)

    def queries_of(h):
        return qfull[h].reshape(ROWS * GROUPED, HD)

    row_request = lax.broadcasted_iota(jnp.int32, (ROWS * GROUPED, HD), 0) // (2 * UNIT)
    lane_request = lax.rem(lax.broadcasted_iota(jnp.int32, (ROWS * GROUPED, HD), 1), REQS)
    meets[...] = jnp.where((grp == 0) | (row_request == lane_request), 1.0, 0.0)

    def attend(h, j):
        mask = jnp.concatenate([meets[...]] * (CHUNK // HD), axis=1)
        for n in range(CHUNKS):
            at = pl.ds(pl.multiple_of((j * CHUNKS + n) * CHUNK, CHUNK), CHUNK)
            scores = lax.dot_general(
                queries_of(h), kh[h, at, :], (((1,), (1,)), ((), ())), preferred_element_type=f32
            )
            weights = (weights_of(scores) * mask).astype(bf16)
            values = jnp.concatenate([vh[h, at, :], ones[at, :]], axis=1)
            acc[h] += jnp.dot(weights, values, preferred_element_type=f32)

    def attend_self(h):
        scores = lax.dot_general(
            queries_of(h), kself[h], (((1,), (1,)), ((), ())), preferred_element_type=f32
        )
        index = lax.broadcasted_iota(jnp.int32, (ROWS * GROUPED, HD), 0)
        row = SHARE * (index // UNIT) + lax.rem(index, SHARE)
        key = SHARE * ctx + lax.broadcasted_iota(jnp.int32, (ROWS * GROUPED, HD), 1)
        allowed = (key <= row) & ((grp == 0) | (index // (2 * UNIT) == ctx // 2))
        weights = jnp.where(allowed, weights_of(scores), 0.0).astype(bf16)
        acc[h] += jnp.dot(weights, vself[h], preferred_element_type=f32)

    def cx3_copy(h):
        return remote(st3.at[h, other], cx3.at[h], cx3_s.at[h], cx3_r.at[h], sibling)

    def rs3_send(h, k):
        return remote(sn3.at[h, k], rs3.at[h, chip], rs3_s, rs3_r.at[h], on_chip(k))

    def rs3_all(h):
        return remote(sn3.at[h, seven], rs3.at[h, seven], rs3_s, rs3_r.at[h], sibling)

    lane8 = lax.broadcasted_iota(jnp.int32, (2 * CHIPS, 8, HD), 2) // 16

    def hand_over(h):
        num = acc[h, :, 0:HD].astype(bf16).reshape(CHIPS, 2, UNIT, HD)
        den = acc[h, :, HD:2 * HD].reshape(2 * CHIPS, 8, 8, HD)
        small = den[:, 0]
        for a in range(1, 8):
            small = jnp.where(lane8 == a, den[:, a], small)
        small = pack_den(small).reshape(CHIPS, 2, 16, HD)
        for p in range(2):
            st3[h, p, :, 0:UNIT, :] = num[:, p]
            st3[h, p, :, UNIT:MSG, :] = small[:, p]
        cx3_copy(h).start()

    def den_of(block):
        return block[:, UNIT:UNIT + 8].astype(f32) + block[:, UNIT + 8:MSG].astype(f32)

    def reduce_cores3(h):
        cx3_copy(h).wait_recv()
        mine = st3[h, core]
        got = cx3[h]
        sn3[h, :, 0:UNIT, :] = (mine[:, 0:UNIT].astype(f32) + got[:, 0:UNIT].astype(f32)).astype(bf16)
        sn3[h, :, UNIT:MSG, :] = pack_den(den_of(mine) + den_of(got))
        rs3[h, chip] = sn3[h, chip]
        for d in range(1, CHIPS):
            rs3_send(h, peer(d)).start()

    def finish_heads(h):
        rs3_all(h).wait_recv()
        got = rs3[h]
        num = jnp.sum(got[:, 0:UNIT].astype(f32), axis=0)
        den = jnp.sum(den_of(got), axis=0)
        wide = jnp.concatenate(
            [jnp.broadcast_to(den[:, 16 * a:16 * a + 1], (8, HD)) for a in range(8)], axis=0)
        hfull[h, chip, core] = (num / wide).astype(bf16)
        share_out(heads_out, h)

    def finish_kv():
        for u in range(4, 8):
            total = total1(u).astype(bf16)
            for half in range(2):
                h = 2 * (u % 2) + half
                piece = total[half * SHARE:(half + 1) * SHARE]
                if u < 6:
                    kself[h, 0:SHARE, :] = piece
                    kvfl[0, pl.ds(h, SHARE, stride=HEADS), :] = piece.astype(f32)
                else:
                    vself[h, 0:SHARE, 0:HD] = piece
                    vself[h, 0:SHARE, HD:2 * HD] = jnp.ones((SHARE, HD), bf16)
                    kvfl[1, pl.ds(h, SHARE, stride=HEADS), :] = piece.astype(f32)
        kvown[...] = kvfl[...].astype(bf16)
        remote(kvown, kvgot, gr_s, gr_r, twin).start()

    def pick_kv():
        remote(kvown, kvgot, gr_s, gr_r, twin).wait_recv()
        kvfull[0, chip, core] = jnp.where(grp == 0, kvown[...].astype(f32), kvgot[...].astype(f32)).astype(bf16)

    kv_store = pltpu.make_async_copy(kvfull.at[0], kv_out, out_sem)

    @pl.loop(0, HEADS * STEPS)
    def _(it):
        h = it // STEPS
        j = lax.rem(it, STEPS)

        @pl.when(it == 1)
        def _():
            for u in range(1, HEADS):
                forward(queries, u)

        @pl.when((h >= 1) & (j == 0))
        def _():
            gathered(queries, h)

        @pl.when(it == 3)
        def _():
            finish_kv()
            attend_self(0)
            hand_over(0)

        @pl.when(it == 4)
        def _():
            reduce_cores3(0)
            reduce_cores3(1)

        @pl.when(it == 6)
        def _():
            reduce_cores3(2)

        @pl.when(it == 5)
        def _():
            pick_kv()
            share_out(new_rows, 0)

        @pl.when((it == 6) | (it == 7))
        def _():
            finish_heads(it - 6)


        attend(h, j)

        @pl.when((h >= 1) & (j == STEPS - 1))
        def _():
            attend_self(h)
            hand_over(h)

    last = HEADS - 1
    half = ROWS // 2

    def project(h):
        heads = hfull[h, :, core]
        lhs = jnp.concatenate(
            [heads[:, 0:SHARE].reshape(half, HD), heads[:, SHARE:UNIT].reshape(half, HD)], axis=1)
        for q, w_ref in enumerate((wo_ref, wo_got)):
            term = lax.dot_general(
                lhs, w_ref[:, h * 256:(h + 1) * 256], (((1,), (1,)), ((), ())), preferred_element_type=f32)
            oacc[q] = term if h == 0 else oacc[q] + term

    reduce_cores3(last)
    finish_heads(last - 1)
    forward(new_rows, 0)
    wo_copy.wait_recv()
    for h in range(last - 1):
        ag_all(heads_out, h).wait_recv()
        project(h)
    finish_heads(last)
    ag_all(heads_out, last - 1).wait_recv()
    project(last - 1)
    ag_all(heads_out, last).wait_recv()
    project(last)
    st5[...] = oacc[...].astype(bf16).reshape(2, 4, UNIT, MODEL)

    def p5_send(q, t):
        return remote(st5.at[q, t], rs5.at[4 * core + tp], p5_s, p5_r,
                      {"ctx": ctx if q == 0 else 2 * chip + other, "tp": t})

    p5_all = remote(rs5.at[seven], rs5.at[seven], p5_s, p5_r, sibling)
    for d in range(1, 4):
        to = lax.rem(tp + d, 4)
        p5_send(0, to).start()
        p5_send(1, to).start()
    p5_send(1, tp).start()
    rs5[4 * core + tp] = st5[0, tp]
    gathered(new_rows, 0)
    kv_store.start()
    p5_all.wait_recv()
    pieces = []
    for p in range(2):
        total = rs5[4 * p].astype(f32)
        for t in range(1, 4):
            total = total + rs5[4 * p + t].astype(f32)
        pieces.append(total)
    out_ref[...] = jnp.concatenate(
        [pieces[0][0:SHARE], pieces[1][0:SHARE], pieces[0][SHARE:UNIT], pieces[1][SHARE:UNIT]], axis=0)

    @pl.loop(0, 8)
    def _(u):
        cx1_copy(u).wait_send()
        rs1_all(u).wait_send()

    @pl.loop(0, HEADS)
    def _(h):
        cx3_copy(h).wait_send()
        rs3_all(h).wait_send()
        shared_done(queries, h)
        ag_all(heads_out, h).wait_send()

    shared_done(new_rows, 0)
    remote(kvown, kvgot, gr_s, gr_r, twin).wait_send()
    wo_copy.wait_send()
    p5_all.wait_send()
    kv_store.wait()


def layer(start, lengths, tok, wq, wk, wv, wo, pool_k, pool_v):
    vmem, dma = pltpu.VMEM, pltpu.SemaphoreType.DMA
    inside = pl.BlockSpec(memory_space=pltpu.VMEM)
    outside = pl.BlockSpec(memory_space=pl.ANY)
    small = pl.BlockSpec(memory_space=pltpu.SMEM)
    share = (2 * HEADS, CHIPS, UNIT, HD)
    msg = (HEADS, CHIPS, MSG, HD)
    return pl.pallas_call(
        layer_kernel,
        name="layer",
        out_shape=(
            jax.ShapeDtypeStruct((ROWS // 4, MODEL), f32),
            jax.ShapeDtypeStruct((CHIPS, 2, 2, SHARE * HEADS, HD), bf16),
        ),
        in_specs=[small, small] + [inside] * 5 + [outside] * 2,
        out_specs=(inside, outside),
        scratch_shapes=[
            vmem((SLOTS_DEV * HEADS, HD), bf16),
            vmem((SLOTS_DEV * HEADS, HD), bf16),
            vmem((PIECE * HEADS, HD), f32),
            vmem((PIECE * HEADS, HD), f32),
            vmem((HEADS, SLOTS_DEV, HD), bf16),
            vmem((HEADS, SLOTS_DEV, HD), bf16),
            vmem((SLOTS_DEV, HD), bf16),
            vmem((HEADS, ROWS * GROUPED, 2 * HD), f32),
            vmem((ROWS * GROUPED, HD), f32),
            vmem((2 * HEADS, 2, CHIPS, UNIT, HD), bf16),
            vmem(share, bf16),
            vmem(share, bf16),
            vmem(share, bf16),
            vmem((HEADS, CHIPS, 2, UNIT, HD), bf16),
            vmem((2, SHARE * HEADS, HD), bf16),
            vmem((2, SHARE * HEADS, HD), bf16),
            vmem((1, CHIPS, 2, 2, SHARE * HEADS, HD), bf16),
            vmem((HEADS, HD, HD), bf16),
            vmem((HEADS, HD, 2 * HD), bf16),
            vmem((2, SHARE * HEADS, HD), f32),
            vmem((HEADS, 2, CHIPS, MSG, HD), bf16),
            vmem(msg, bf16),
            vmem(msg, bf16),
            vmem(msg, bf16),
            vmem((HEADS, CHIPS, 2, UNIT, HD), bf16),
            vmem((MODEL, HEADS * GROUPED * HD), bf16),
            vmem((2, ROWS // 2, MODEL), f32),
            vmem((2, 4, UNIT, MODEL), bf16),
            vmem((8, UNIT, MODEL), bf16),
            dma((2, SLOTS_DEV // DEINT)),
            dma(()),
            dma((8,)), dma((8,)),
            dma(()), dma((8,)),
            dma(()), dma((HEADS,)), dma((HEADS,)), dma((HEADS,)),
            dma(()), dma((1,)), dma((1,)), dma((1,)),
            dma(()), dma((HEADS,)),
            dma(()), dma(()),
            dma(()), dma(()),
            dma((HEADS,)), dma((HEADS,)),
            dma(()), dma((HEADS,)),
            dma(()), dma(()),
        ],
        compiler_params=pltpu.CompilerParams(
            collective_id=0, has_side_effects=True, vmem_limit_bytes=60 * 2**20),
        cost_estimate=pl.CostEstimate(
            flops=22 * 10**9, bytes_accessed=14 * 2**20, transcendentals=42 * 10**6),
    )(start, lengths, tok, wq, wk, wv, wo, pool_k, pool_v)


COPIES = 8


def store_kernel(
    start_ref, dest_ref, attn, kv, pool_k, pool_v, attn_out, keys_out, values_out, held, rows, kv_sem, in_sem, copy_sem, row_sem
):
    grp = lax.axis_index("grp")
    first = lax.axis_index("ctx") * SLOTS_DEV
    span = SLOTS_DEV // COPIES

    def fetch(which, i):
        at = pl.ds(i * span, span)
        return pltpu.make_async_copy((pool_k, pool_v)[which].at[at], held.at[which, at], in_sem.at[which, i])

    def put(which, i):
        at = pl.ds(i * span, span)
        return pltpu.make_async_copy(held.at[which, at], (keys_out, values_out)[which].at[at], copy_sem.at[which, i])

    for i in range(COPIES):
        for which in range(2):
            fetch(which, i).start()
    take = pltpu.make_async_copy(kv, rows, kv_sem)
    take.start()
    attn_out[...] = attn[...].T.astype(bf16)
    for i in range(COPIES):
        for which in range(2):
            fetch(which, i).wait()
            put(which, i).start()
    for i in range(COPIES):
        for which in range(2):
            put(which, i).wait()
    take.wait()

    def slot(b):
        return jnp.where(grp == 0, start_ref[0] + b * BLK, dest_ref[b] * BLK) - first

    def block(b, which):
        dst = (keys_out, values_out)[which]
        return pltpu.make_async_copy(
            rows.at[b // 4, lax.rem(b // 2, 2), which, pl.ds(lax.rem(b, 2) * BLK, BLK)],
            dst.at[pl.ds(slot(b), BLK)], row_sem.at[which, b])

    def inside(b):
        at = slot(b)
        return (at >= 0) & (at <= SLOTS_DEV - BLK)

    def across(b):
        at = slot(b)
        return ((at > -BLK) & (at < 0)) | ((at > SLOTS_DEV - BLK) & (at < SLOTS_DEV))

    blocks = ROWS // BLK

    @pl.loop(0, blocks)
    def _(b):
        @pl.when(inside(b))
        def _():
            block(b, 0).start()
            block(b, 1).start()

        @pl.when(across(b))
        def _():
            @pl.loop(0, BLK)
            def _(i):
                at = slot(b) + i

                @pl.when((at >= 0) & (at < SLOTS_DEV))
                def _():
                    for which in range(2):
                        row = pltpu.make_async_copy(
                            rows.at[b // 4, lax.rem(b // 2, 2), which,
                                  pl.ds(lax.rem(b, 2) * BLK + i, 1)],
                            (keys_out, values_out)[which].at[pl.ds(at, 1)],
                            row_sem.at[which, b])
                        row.start()
                        row.wait()

    @pl.loop(0, blocks)
    def _(b):
        @pl.when(inside(b))
        def _():
            block(b, 0).wait()
            block(b, 1).wait()


def store(start, dest_blocks, attn, kv, pool_k, pool_v):
    dma = pltpu.SemaphoreType.DMA
    inside = pl.BlockSpec(memory_space=pltpu.VMEM)
    outside = pl.BlockSpec(memory_space=pl.ANY)
    small = pl.BlockSpec(memory_space=pltpu.SMEM)
    shape = jax.ShapeDtypeStruct((SLOTS_DEV, HEADS, HD), bf16)
    return pl.pallas_call(
        store_kernel,
        name="store",
        out_shape=(jax.ShapeDtypeStruct((MODEL, ROWS // 4), bf16), shape, shape),
        in_specs=[small, small, inside] + [outside] * 3,
        out_specs=(inside, outside, outside),
        scratch_shapes=[
            pltpu.VMEM((2, SLOTS_DEV, HEADS, HD), bf16),
            pltpu.VMEM(kv.shape, bf16), dma(()),
            dma((2, COPIES)), dma((2, COPIES)), dma((2, ROWS // BLK))],
        compiler_params=pltpu.CompilerParams(vmem_limit_bytes=60 * 2**20),
        cost_estimate=pl.CostEstimate(flops=0, bytes_accessed=21 * 2**20, transcendentals=0),
    )(start, dest_blocks, attn, kv, pool_k, pool_v)


def body(
    new_tokens, w_query, w_key, w_value, w_out, pool_keys, pool_values, stretch_start, lengths, dest_blocks
):
    flat = (SLOTS_DEV * HEADS, HD)
    pool_k = pool_keys.reshape(flat)
    pool_v = pool_values.reshape(flat)
    out, kv = layer(
        stretch_start, lengths, new_tokens[0].T, w_query, w_key, w_value, w_out.T, pool_k, pool_v)
    kv = kv.reshape(CHIPS, 2, 2, SHARE, HEADS, HD)
    attn_out, keys_out, values_out = store(
        stretch_start, dest_blocks, out, kv, pool_keys[0], pool_values[0])
    return attn_out.T[None], keys_out[None], values_out[None]


def solution(mesh):
    return jax.shard_map(
        body,
        mesh=mesh,
        in_specs=(
            P("grp", None, "ctx"),
            P("ctx", "tp"),
            P("ctx", "tp"),
            P("ctx", "tp"),
            P("tp", "ctx"),
            P("grp", "ctx", "tp", None),
            P("grp", "ctx", "tp", None),
            P(),
            P(),
            P(),
        ),
        out_specs=(P("grp", "tp", "ctx"), P("grp", "ctx", "tp", None), P("grp", "ctx", "tp", None)),
        check_vma=False,
    )
```

```python
import jax
import jax.numpy as jnp
from jax import lax
from jax.experimental import pallas as pl
from jax.experimental.pallas import tpu as pltpu
from jax.sharding import PartitionSpec as P

HD = 128
GROUPED = 2
BLK = 16
REQS = 8
ROWS = 512
SLOTS_DEV = 5120
HEADS = 4
CHIPS = 8
SHARE = 32
UNIT = GROUPED * SHARE
MSG = UNIT + 16
DEINT = 512
PIECE = 128
CHUNK = 512
CHUNKS = 5
STEPS = SLOTS_DEV // (CHUNK * CHUNKS)
MODEL = 288
LOG2E = 1.4426950408889634

soft_cap = 50.0
query_scale = 1.0 / 12.0
bf16 = jnp.bfloat16
f32 = jnp.float32


def weights_of(scores):
    return jnp.exp2(jnp.tanh(scores * (1.0 / soft_cap)) * (soft_cap * LOG2E))


def pack_den(den):
    high = den.astype(bf16)
    low = (den - high.astype(f32)).astype(bf16)
    return jnp.concatenate([high, low], axis=-2)


def layer_kernel(
    start_ref, len_ref, tok_ref, wq_ref, wk_ref, wv_ref, wo_ref, pool_k, pool_v,
    out_ref, kv_out,
    kbuf, vbuf, kfl, vfl, kh, vh, ones, acc, meets,
    st1, cx1, sn1, rs1, qfull, kvown, kvgot, kvfull, kself, vself, kvfl,
    st3, cx3, sn3, rs3, hfull, wo_got, oacc, st5, rs5,
    in_sem, out_sem, cx1_s, cx1_r, rs1_s, rs1_r, agq_s, agq_r, fwq_s, fwq_r, agk_s, agk_r, fwk_s, fwk_r,
    agh_s, agh_r, gr_s, gr_r, wo_s, wo_r,
    cx3_s, cx3_r, rs3_s, rs3_r, p5_s, p5_r,
):
    ctx = lax.axis_index("ctx")
    tp = lax.axis_index("tp")
    grp = lax.axis_index("grp")
    chip = ctx // 2
    core = lax.rem(ctx, 2)
    other = 1 - core
    sibling = {"ctx": 2 * chip + other}
    twin = {"grp": 1 - grp}

    def peer(d):
        return lax.rem(chip + d, CHIPS)

    def on_chip(k):
        return {"ctx": 2 * k + core}

    def remote(src, dst, send, recv, device):
        return pltpu.make_async_remote_copy(
            src_ref=src, dst_ref=dst, send_sem=send, recv_sem=recv, device_id=device,
            device_id_type=pl.DeviceIdType.MESH,
        )

    rows = DEINT * HEADS
    parts = SLOTS_DEV // DEINT

    def pool_in(j, which):
        src, dst = ((pool_k, kbuf), (pool_v, vbuf))[which]
        at = pl.ds(pl.multiple_of(j * rows, rows), rows)
        return pltpu.make_async_copy(src.at[at], dst.at[at], in_sem.at[which, j])

    @pl.loop(0, parts)
    def _(j):
        pool_in(j, 0).start()
        pool_in(j, 1).start()

    barrier = pltpu.get_barrier_semaphore()

    def greet(device):
        pl.semaphore_signal(barrier, inc=1, device_id=device, device_id_type=pl.DeviceIdType.MESH)

    greet(sibling)
    greet(twin)
    for d in range(1, CHIPS):
        greet(on_chip(peer(d)))
    for d in range(1, 4):
        greet({"tp": lax.rem(tp + d, 4)})
        greet({"ctx": 2 * chip + other, "tp": lax.rem(tp + d, 4)})

    def cx1_copy(u):
        return remote(st1.at[u, other], cx1.at[u], cx1_s.at[u], cx1_r.at[u], sibling)

    seven = pl.ds(0, CHIPS - 1)

    def rs1_send(u, k):
        return remote(sn1.at[u, k], rs1.at[u, chip], rs1_s, rs1_r.at[u], on_chip(k))

    def rs1_all(u):
        return remote(sn1.at[u, seven], rs1.at[u, seven], rs1_s, rs1_r.at[u], sibling)

    def ag_send(buf, u, k):
        ref, send, recv, _, _ = buf
        return remote(ref.at[u, chip, core], ref.at[u, chip, core], send, recv.at[u], on_chip(k))

    def ag_all(buf, u):
        ref, send, recv, _, _ = buf
        return remote(ref.at[u, seven, core], ref.at[u, seven, core], send, recv.at[u], sibling)

    def fw_send(buf, u):
        ref, _, _, send, recv = buf
        return remote(ref.at[u, :, core], ref.at[u, :, core], send.at[u], recv.at[u], sibling)

    def share_out(buf, u):
        for d in range(1, CHIPS):
            ag_send(buf, u, peer(d)).start()

    def forward(buf, u):
        ag_all(buf, u).wait_recv()
        fw_send(buf, u).start()

    def gathered(buf, u):
        ref, _, _, send, recv = buf
        remote(ref.at[u, :, other], ref.at[u, :, other], send.at[u], recv.at[u], sibling).wait_recv()

    def shared_done(buf, u):
        ag_all(buf, u).wait_send()
        fw_send(buf, u).wait_send()

    queries = (qfull, agq_s, agq_r, fwq_s, fwq_r)
    new_rows = (kvfull, agk_s, agk_r, fwk_s, fwk_r)
    heads_out = (hfull, agh_s, agh_r, None, None)

    wo_copy = remote(wo_ref, wo_got, wo_s, wo_r, sibling)

    def project_in(w_ref, first):
        part = lax.dot_general(
            tok_ref[...], w_ref[...], (((0,), (0,)), ((), ())), preferred_element_type=f32
        ).astype(bf16)
        for n in range(part.shape[1] // HD):
            piece = part[:, n * HD:(n + 1) * HD].reshape(CHIPS, 2, SHARE, HD)
            u, g = first + n // 2, n % 2
            for p in range(2):
                st1[u, p, :, g * SHARE:(g + 1) * SHARE, :] = piece[:, p]

    project_in(wq_ref, 0)
    pl.semaphore_wait(barrier, 2 + CHIPS - 1 + 6)
    for u in range(4):
        cx1_copy(u).start()
    project_in(wk_ref, 4)
    project_in(wv_ref, 6)
    for u in range(4, 8):
        cx1_copy(u).start()
    wo_copy.start()

    def reduce_cores(u):
        cx1_copy(u).wait_recv()
        both = (st1[u, core].astype(f32) + cx1[u].astype(f32)).astype(bf16)
        sn1[u] = both
        rs1[u, chip] = sn1[u, chip]
        for d in range(1, CHIPS):
            rs1_send(u, peer(d)).start()

    def total1(u):
        rs1_all(u).wait_recv()
        total = rs1[u, 0].astype(f32)
        for k in range(1, CHIPS):
            total = total + rs1[u, k].astype(f32)
        return total

    def finish_query(u):
        qfull[u, chip, core] = (total1(u) * query_scale).astype(bf16)
        share_out(queries, u)

    lane_row = lax.broadcasted_iota(jnp.int32, (REQS, HD), 0)
    limits = jnp.zeros((REQS, HD), jnp.int32)
    for r in range(REQS):
        limits = jnp.where(lane_row == r, len_ref[r], limits)
    limits = jnp.where(grp == 0, start_ref[0] - ctx * SLOTS_DEV - lane_row, limits - ctx)
    plane_step = jnp.where(grp == 0, REQS, 16)
    piece_planes = PIECE // REQS
    plane_of = lax.broadcasted_iota(jnp.int32, (piece_planes, REQS, HD), 0) * plane_step

    def deint(j):
        pool_in(j, 0).wait()
        pool_in(j, 1).wait()

        @pl.loop(0, DEINT // PIECE)
        def _(i):
            first = j * DEINT + i * PIECE
            at = pl.ds(pl.multiple_of(first * HEADS, PIECE * HEADS), PIECE * HEADS)
            to = pl.ds(pl.multiple_of(first, PIECE), PIECE)
            kfl[...] = kbuf[at].astype(f32)
            vfl[...] = vbuf[at].astype(f32)
            planes = plane_of + (first // REQS) * plane_step
            seen = jnp.where(planes < limits[None], 1.0, 0.0).reshape(PIECE, HD)
            ones[to, :] = seen.astype(bf16)
            for h in range(HEADS):
                kh[h, to, :] = kfl[pl.ds(h, PIECE, stride=HEADS)].astype(bf16)
                vh[h, to, :] = (vfl[pl.ds(h, PIECE, stride=HEADS)] * seen).astype(bf16)

    def deint_range(first, last):
        @pl.loop(first, last)
        def _(j):
            deint(j)

    deint_range(0, 1)
    for u in range(4):
        reduce_cores(u)
    deint_range(1, 4)
    finish_query(0)
    finish_query(1)
    deint_range(4, 5)
    finish_query(2)
    finish_query(3)
    deint_range(5, 6)
    for u in range(4, 8):
        reduce_cores(u)
    forward(queries, 0)
    deint_range(6, parts)
    acc[...] = jnp.zeros_like(acc)
    kself[...] = jnp.zeros_like(kself)
    vself[...] = jnp.zeros_like(vself)
    gathered(queries, 0)

    def queries_of(h):
        return qfull[h].reshape(ROWS * GROUPED, HD)

    row_request = lax.broadcasted_iota(jnp.int32, (ROWS * GROUPED, HD), 0) // (2 * UNIT)
    lane_request = lax.rem(lax.broadcasted_iota(jnp.int32, (ROWS * GROUPED, HD), 1), REQS)
    meets[...] = jnp.where((grp == 0) | (row_request == lane_request), 1.0, 0.0)

    def attend(h, j):
        mask = jnp.concatenate([meets[...]] * (CHUNK // HD), axis=1)
        for n in range(CHUNKS):
            at = pl.ds(pl.multiple_of((j * CHUNKS + n) * CHUNK, CHUNK), CHUNK)
            scores = lax.dot_general(
                queries_of(h), kh[h, at, :], (((1,), (1,)), ((), ())), preferred_element_type=f32
            )
            weights = (weights_of(scores) * mask).astype(bf16)
            values = jnp.concatenate([vh[h, at, :], ones[at, :]], axis=1)
            acc[h] += jnp.dot(weights, values, preferred_element_type=f32)

    def attend_self(h):
        scores = lax.dot_general(
            queries_of(h), kself[h], (((1,), (1,)), ((), ())), preferred_element_type=f32
        )
        index = lax.broadcasted_iota(jnp.int32, (ROWS * GROUPED, HD), 0)
        row = SHARE * (index // UNIT) + lax.rem(index, SHARE)
        key = SHARE * ctx + lax.broadcasted_iota(jnp.int32, (ROWS * GROUPED, HD), 1)
        allowed = (key <= row) & ((grp == 0) | (index // (2 * UNIT) == ctx // 2))
        weights = jnp.where(allowed, weights_of(scores), 0.0).astype(bf16)
        acc[h] += jnp.dot(weights, vself[h], preferred_element_type=f32)

    def cx3_copy(h):
        return remote(st3.at[h, other], cx3.at[h], cx3_s.at[h], cx3_r.at[h], sibling)

    def rs3_send(h, k):
        return remote(sn3.at[h, k], rs3.at[h, chip], rs3_s, rs3_r.at[h], on_chip(k))

    def rs3_all(h):
        return remote(sn3.at[h, seven], rs3.at[h, seven], rs3_s, rs3_r.at[h], sibling)

    lane8 = lax.broadcasted_iota(jnp.int32, (2 * CHIPS, 8, HD), 2) // 16

    def hand_over(h):
        num = acc[h, :, 0:HD].astype(bf16).reshape(CHIPS, 2, UNIT, HD)
        den = acc[h, :, HD:2 * HD].reshape(2 * CHIPS, 8, 8, HD)
        small = den[:, 0]
        for a in range(1, 8):
            small = jnp.where(lane8 == a, den[:, a], small)
        small = pack_den(small).reshape(CHIPS, 2, 16, HD)
        for p in range(2):
            st3[h, p, :, 0:UNIT, :] = num[:, p]
            st3[h, p, :, UNIT:MSG, :] = small[:, p]
        cx3_copy(h).start()

    def den_of(block):
        return block[:, UNIT:UNIT + 8].astype(f32) + block[:, UNIT + 8:MSG].astype(f32)

    def reduce_cores3(h):
        cx3_copy(h).wait_recv()
        mine = st3[h, core]
        got = cx3[h]
        sn3[h, :, 0:UNIT, :] = (mine[:, 0:UNIT].astype(f32) + got[:, 0:UNIT].astype(f32)).astype(bf16)
        sn3[h, :, UNIT:MSG, :] = pack_den(den_of(mine) + den_of(got))
        rs3[h, chip] = sn3[h, chip]
        for d in range(1, CHIPS):
            rs3_send(h, peer(d)).start()

    def finish_heads(h):
        rs3_all(h).wait_recv()
        got = rs3[h]
        num = jnp.sum(got[:, 0:UNIT].astype(f32), axis=0)
        den = jnp.sum(den_of(got), axis=0)
        wide = jnp.concatenate(
            [jnp.broadcast_to(den[:, 16 * a:16 * a + 1], (8, HD)) for a in range(8)], axis=0)
        hfull[h, chip, core] = (num / wide).astype(bf16)
        share_out(heads_out, h)

    def finish_kv():
        for u in range(4, 8):
            total = total1(u).astype(bf16)
            for half in range(2):
                h = 2 * (u % 2) + half
                piece = total[half * SHARE:(half + 1) * SHARE]
                if u < 6:
                    kself[h, 0:SHARE, :] = piece
                    kvfl[0, pl.ds(h, SHARE, stride=HEADS), :] = piece.astype(f32)
                else:
                    vself[h, 0:SHARE, 0:HD] = piece
                    vself[h, 0:SHARE, HD:2 * HD] = jnp.ones((SHARE, HD), bf16)
                    kvfl[1, pl.ds(h, SHARE, stride=HEADS), :] = piece.astype(f32)
        kvown[...] = kvfl[...].astype(bf16)
        remote(kvown, kvgot, gr_s, gr_r, twin).start()

    def pick_kv():
        remote(kvown, kvgot, gr_s, gr_r, twin).wait_recv()
        kvfull[0, chip, core] = jnp.where(grp == 0, kvown[...].astype(f32), kvgot[...].astype(f32)).astype(bf16)

    kv_store = pltpu.make_async_copy(kvfull.at[0], kv_out, out_sem)

    @pl.loop(0, HEADS * STEPS)
    def _(it):
        h = it // STEPS
        j = lax.rem(it, STEPS)

        @pl.when(it == 1)
        def _():
            for u in range(1, HEADS):
                forward(queries, u)

        @pl.when((h >= 1) & (j == 0))
        def _():
            gathered(queries, h)

        @pl.when(it == 3)
        def _():
            finish_kv()
            attend_self(0)
            hand_over(0)

        @pl.when(it == 4)
        def _():
            reduce_cores3(0)
            reduce_cores3(1)

        @pl.when(it == 6)
        def _():
            reduce_cores3(2)

        @pl.when(it == 5)
        def _():
            pick_kv()
            share_out(new_rows, 0)

        @pl.when((it == 6) | (it == 7))
        def _():
            finish_heads(it - 6)


        attend(h, j)

        @pl.when((h >= 1) & (j == STEPS - 1))
        def _():
            attend_self(h)
            hand_over(h)

    last = HEADS - 1
    half = ROWS // 2

    def project(h):
        heads = hfull[h, :, core]
        lhs = jnp.concatenate(
            [heads[:, 0:SHARE].reshape(half, HD), heads[:, SHARE:UNIT].reshape(half, HD)], axis=1)
        for q, w_ref in enumerate((wo_ref, wo_got)):
            term = lax.dot_general(
                lhs, w_ref[:, h * 256:(h + 1) * 256], (((1,), (1,)), ((), ())), preferred_element_type=f32)
            oacc[q] = term if h == 0 else oacc[q] + term

    reduce_cores3(last)
    finish_heads(last - 1)
    forward(new_rows, 0)
    wo_copy.wait_recv()
    for h in range(last - 1):
        ag_all(heads_out, h).wait_recv()
        project(h)
    finish_heads(last)
    ag_all(heads_out, last - 1).wait_recv()
    project(last - 1)
    ag_all(heads_out, last).wait_recv()
    project(last)
    st5[...] = oacc[...].astype(bf16).reshape(2, 4, UNIT, MODEL)

    def p5_send(q, t):
        return remote(st5.at[q, t], rs5.at[4 * core + tp], p5_s, p5_r,
                      {"ctx": ctx if q == 0 else 2 * chip + other, "tp": t})

    p5_all = remote(rs5.at[seven], rs5.at[seven], p5_s, p5_r, sibling)
    for d in range(1, 4):
        to = lax.rem(tp + d, 4)
        p5_send(0, to).start()
        p5_send(1, to).start()
    p5_send(1, tp).start()
    rs5[4 * core + tp] = st5[0, tp]
    gathered(new_rows, 0)
    kv_store.start()
    p5_all.wait_recv()
    pieces = []
    for p in range(2):
        total = rs5[4 * p].astype(f32)
        for t in range(1, 4):
            total = total + rs5[4 * p + t].astype(f32)
        pieces.append(total)
    out_ref[...] = jnp.concatenate(
        [pieces[0][0:SHARE], pieces[1][0:SHARE], pieces[0][SHARE:UNIT], pieces[1][SHARE:UNIT]], axis=0)

    @pl.loop(0, 8)
    def _(u):
        cx1_copy(u).wait_send()
        rs1_all(u).wait_send()

    @pl.loop(0, HEADS)
    def _(h):
        cx3_copy(h).wait_send()
        rs3_all(h).wait_send()
        shared_done(queries, h)
        ag_all(heads_out, h).wait_send()

    shared_done(new_rows, 0)
    remote(kvown, kvgot, gr_s, gr_r, twin).wait_send()
    wo_copy.wait_send()
    p5_all.wait_send()
    kv_store.wait()


def layer(start, lengths, tok, wq, wk, wv, wo, pool_k, pool_v):
    vmem, dma = pltpu.VMEM, pltpu.SemaphoreType.DMA
    inside = pl.BlockSpec(memory_space=pltpu.VMEM)
    outside = pl.BlockSpec(memory_space=pl.ANY)
    small = pl.BlockSpec(memory_space=pltpu.SMEM)
    share = (2 * HEADS, CHIPS, UNIT, HD)
    msg = (HEADS, CHIPS, MSG, HD)
    return pl.pallas_call(
        layer_kernel,
        name="layer",
        out_shape=(
            jax.ShapeDtypeStruct((ROWS // 4, MODEL), f32),
            jax.ShapeDtypeStruct((CHIPS, 2, 2, SHARE * HEADS, HD), bf16),
        ),
        in_specs=[small, small] + [inside] * 5 + [outside] * 2,
        out_specs=(inside, outside),
        scratch_shapes=[
            vmem((SLOTS_DEV * HEADS, HD), bf16),
            vmem((SLOTS_DEV * HEADS, HD), bf16),
            vmem((PIECE * HEADS, HD), f32),
            vmem((PIECE * HEADS, HD), f32),
            vmem((HEADS, SLOTS_DEV, HD), bf16),
            vmem((HEADS, SLOTS_DEV, HD), bf16),
            vmem((SLOTS_DEV, HD), bf16),
            vmem((HEADS, ROWS * GROUPED, 2 * HD), f32),
            vmem((ROWS * GROUPED, HD), f32),
            vmem((2 * HEADS, 2, CHIPS, UNIT, HD), bf16),
            vmem(share, bf16),
            vmem(share, bf16),
            vmem(share, bf16),
            vmem((HEADS, CHIPS, 2, UNIT, HD), bf16),
            vmem((2, SHARE * HEADS, HD), bf16),
            vmem((2, SHARE * HEADS, HD), bf16),
            vmem((1, CHIPS, 2, 2, SHARE * HEADS, HD), bf16),
            vmem((HEADS, HD, HD), bf16),
            vmem((HEADS, HD, 2 * HD), bf16),
            vmem((2, SHARE * HEADS, HD), f32),
            vmem((HEADS, 2, CHIPS, MSG, HD), bf16),
            vmem(msg, bf16),
            vmem(msg, bf16),
            vmem(msg, bf16),
            vmem((HEADS, CHIPS, 2, UNIT, HD), bf16),
            vmem((MODEL, HEADS * GROUPED * HD), bf16),
            vmem((2, ROWS // 2, MODEL), f32),
            vmem((2, 4, UNIT, MODEL), bf16),
            vmem((8, UNIT, MODEL), bf16),
            dma((2, SLOTS_DEV // DEINT)),
            dma(()),
            dma((8,)), dma((8,)),
            dma(()), dma((8,)),
            dma(()), dma((HEADS,)), dma((HEADS,)), dma((HEADS,)),
            dma(()), dma((1,)), dma((1,)), dma((1,)),
            dma(()), dma((HEADS,)),
            dma(()), dma(()),
            dma(()), dma(()),
            dma((HEADS,)), dma((HEADS,)),
            dma(()), dma((HEADS,)),
            dma(()), dma(()),
        ],
        compiler_params=pltpu.CompilerParams(
            collective_id=0, has_side_effects=True, vmem_limit_bytes=60 * 2**20),
        cost_estimate=pl.CostEstimate(
            flops=22 * 10**9, bytes_accessed=14 * 2**20, transcendentals=42 * 10**6),
    )(start, lengths, tok, wq, wk, wv, wo, pool_k, pool_v)


COPIES = 4


def store_kernel(
    start_ref, dest_ref, attn, kv, pool_k, pool_v, attn_out, keys_out, values_out, held, rows, kv_sem, in_sem, copy_sem, row_sem
):
    grp = lax.axis_index("grp")
    first = lax.axis_index("ctx") * SLOTS_DEV
    span = SLOTS_DEV // COPIES

    def fetch(which, i):
        at = pl.ds(i * span, span)
        return pltpu.make_async_copy((pool_k, pool_v)[which].at[at], held.at[which, at], in_sem.at[which, i])

    def put(which, i):
        at = pl.ds(i * span, span)
        return pltpu.make_async_copy(held.at[which, at], (keys_out, values_out)[which].at[at], copy_sem.at[which, i])

    for i in range(COPIES):
        for which in range(2):
            fetch(which, i).start()
    take = pltpu.make_async_copy(kv, rows, kv_sem)
    take.start()
    attn_out[...] = attn[...].T.astype(bf16)
    for i in range(COPIES):
        for which in range(2):
            fetch(which, i).wait()
            put(which, i).start()
    for i in range(COPIES):
        for which in range(2):
            put(which, i).wait()
    take.wait()

    def slot(b):
        return jnp.where(grp == 0, start_ref[0] + b * BLK, dest_ref[b] * BLK) - first

    def block(b, which):
        dst = (keys_out, values_out)[which]
        return pltpu.make_async_copy(
            rows.at[b // 4, lax.rem(b // 2, 2), which, pl.ds(lax.rem(b, 2) * BLK, BLK)],
            dst.at[pl.ds(slot(b), BLK)], row_sem.at[which])

    def inside(b):
        at = slot(b)
        return (at >= 0) & (at <= SLOTS_DEV - BLK)

    def across(b):
        at = slot(b)
        return ((at > -BLK) & (at < 0)) | ((at > SLOTS_DEV - BLK) & (at < SLOTS_DEV))

    blocks = ROWS // BLK

    @pl.loop(0, blocks)
    def _(b):
        @pl.when(inside(b))
        def _():
            block(b, 0).start()
            block(b, 1).start()

        @pl.when(across(b))
        def _():
            @pl.loop(0, BLK)
            def _(i):
                at = slot(b) + i

                @pl.when((at >= 0) & (at < SLOTS_DEV))
                def _():
                    for which in range(2):
                        row = pltpu.make_async_copy(
                            rows.at[b // 4, lax.rem(b // 2, 2), which,
                                  pl.ds(lax.rem(b, 2) * BLK + i, 1)],
                            (keys_out, values_out)[which].at[pl.ds(at, 1)],
                            row_sem.at[which])
                        row.start()
                        row.wait()

    @pl.loop(0, blocks)
    def _(b):
        @pl.when(inside(b))
        def _():
            block(b, 0).wait()
            block(b, 1).wait()


def store(start, dest_blocks, attn, kv, pool_k, pool_v):
    dma = pltpu.SemaphoreType.DMA
    inside = pl.BlockSpec(memory_space=pltpu.VMEM)
    outside = pl.BlockSpec(memory_space=pl.ANY)
    small = pl.BlockSpec(memory_space=pltpu.SMEM)
    shape = jax.ShapeDtypeStruct((SLOTS_DEV, HEADS, HD), bf16)
    return pl.pallas_call(
        store_kernel,
        name="store",
        out_shape=(jax.ShapeDtypeStruct((MODEL, ROWS // 4), bf16), shape, shape),
        in_specs=[small, small, inside] + [outside] * 3,
        out_specs=(inside, outside, outside),
        scratch_shapes=[
            pltpu.VMEM((2, SLOTS_DEV, HEADS, HD), bf16),
            pltpu.VMEM(kv.shape, bf16), dma(()),
            dma((2, COPIES)), dma((2, COPIES)), dma((2,))],
        compiler_params=pltpu.CompilerParams(vmem_limit_bytes=60 * 2**20),
        cost_estimate=pl.CostEstimate(flops=0, bytes_accessed=21 * 2**20, transcendentals=0),
    )(start, dest_blocks, attn, kv, pool_k, pool_v)


def body(
    new_tokens, w_query, w_key, w_value, w_out, pool_keys, pool_values, stretch_start, lengths, dest_blocks
):
    flat = (SLOTS_DEV * HEADS, HD)
    pool_k = pool_keys.reshape(flat)
    pool_v = pool_values.reshape(flat)
    out, kv = layer(
        stretch_start, lengths, new_tokens[0].T, w_query, w_key, w_value, w_out.T, pool_k, pool_v)
    kv = kv.reshape(CHIPS, 2, 2, SHARE, HEADS, HD)
    attn_out, keys_out, values_out = store(
        stretch_start, dest_blocks, out, kv, pool_keys[0], pool_values[0])
    return attn_out.T[None], keys_out[None], values_out[None]


def solution(mesh):
    return jax.shard_map(
        body,
        mesh=mesh,
        in_specs=(
            P("grp", None, "ctx"),
            P("ctx", "tp"),
            P("ctx", "tp"),
            P("ctx", "tp"),
            P("tp", "ctx"),
            P("grp", "ctx", "tp", None),
            P("grp", "ctx", "tp", None),
            P(),
            P(),
            P(),
        ),
        out_specs=(P("grp", "tp", "ctx"), P("grp", "ctx", "tp", None), P("grp", "ctx", "tp", None)),
        check_vma=False,
    )
```
